32 devices in a mesh: gx: 8 (over z, x), gy: 4 (over y, core).
Axes of the slice: x: 2, y: 2, z: 4, core: 2. Of those that a mesh axis runs over, the one named last changes fastest.
Arguments:
- blocks: float32 [8, 4, 64, 4, 128], P('gx', 'gy'), may hold values from 0 to 1, as said below
- active_counts: int32 [8, 4], P('gx', 'gy'), may hold values from 1 to 32, as said below
- pair_lists: int32 [8, 4, 32, 16], P('gx', 'gy'), may hold values from 0 to 575
- cell_ids: int32 [8, 4, 64], P('gx', 'gy'), may hold values from 0 to 15, as said below
Outputs:
- accel: float32 [8, 4, 32, 3, 128], P('gx', 'gy')
The draws below stay inside these ranges and needn't reach their ends.
Inputs may be any that keep to these rules, and one draw needn't show every extreme that they name: `active_counts`: every domain has at least one active block and some domain has 32; the active blocks are the first ones of the domain. `pair_lists`: entry (3 a + b) * 64 + n names block n of the domain a - 1 steps along gx and b - 1 steps along gy, with wrap around; a list may repeat a block or name the target block itself. `cell_ids`: A block of domain (i, j) lies in one of the 2 cells (g * 2 + h) with g = (i // 2) * (4 // 2) + j // 2. `blocks`: coordinates lie in [0, 1); masses are positive.
All inputs are finite; a program needn't handle non-finite values.
Results may differ from the reference program's by a relative error of at most 0.0003.
Values sent between devices are 32-bit elements; how exact they have to be, the bound alone decides.
No kernel may reach another device: no remote copies, remote signals or barrier semaphores. Data moves between devices by JAX's collectives and lax.ppermute only.
A program may use at most 64 MiB of HBM per device.

```python
import jax
import jax.numpy as jnp
from jax import lax

BLOCK = 128
NB = 64
ACT = 32
KLIST = 16
SUBC = 2
N_GX = 8
N_GY = 4


def draw_blocks(key, part):
    key_pos = jax.random.fold_in(key, 11)
    key_mass = jax.random.fold_in(key, 12)
    shape_pos = (N_GX, N_GY, NB, 3, BLOCK)
    shape_mass = (N_GX, N_GY, NB, 1, BLOCK)
    position = jax.random.uniform(key_pos, shape_pos, jnp.float32)
    mass = jnp.exp(jax.random.uniform(key_mass, shape_mass, jnp.float32, jnp.log(0.5), jnp.log(2.0))) / (BLOCK * KLIST)
    return jnp.concatenate([position, mass], axis=3).astype(jnp.float32)


def draw_active_counts(key, part):
    counts = jax.random.randint(jax.random.fold_in(key, 21), (N_GX * N_GY,), 1, ACT + 1)
    where = jax.random.randint(jax.random.fold_in(key, 22), (), 0, N_GX * N_GY)
    counts = counts.at[where].set(ACT)
    return counts.reshape(N_GX, N_GY).astype(jnp.int32)


def draw_cell_ids(key, part):
    sub_cell = jax.random.randint(jax.random.fold_in(key, 31), (N_GX, N_GY, NB), 0, SUBC)
    row = jnp.arange(N_GX, dtype=jnp.int32)[:, None, None]
    col = jnp.arange(N_GY, dtype=jnp.int32)[None, :, None]
    group = row // 2 * (N_GY // 2) + col // 2
    return (group * SUBC + sub_cell).astype(jnp.int32)


def set_ends(entries, key, smallest, top_value):
    extent = entries.shape
    index_at = [jax.random.randint(jax.random.fold_in(key, axis), (), 0, extent[axis]) for axis in range(len(extent))]
    entries = entries.at[tuple(index_at)].set(smallest)
    longest = extent.index(max(extent))
    index_at[longest] = (index_at[longest] + 1) % extent[longest]
    return entries.at[tuple(index_at)].set(top_value)


def setup_inputs(seed: int = 0) -> dict:
    key_list = jax.random.split(jax.random.key(seed), 5)
    blocks = draw_blocks(jax.random.fold_in(key_list[4], 71), 0)
    active_counts = draw_active_counts(jax.random.fold_in(key_list[4], 71), 0)
    pair_lists = set_ends(jax.random.randint(key_list[2], (N_GX, N_GY, ACT, KLIST), 0, 9 * NB), jax.random.fold_in(key_list[2], 1), 0, (9 * NB) - 1).astype(jnp.int32)
    cell_ids = draw_cell_ids(jax.random.fold_in(key_list[4], 71), 0)
    return dict(blocks=blocks, active_counts=active_counts, pair_lists=pair_lists, cell_ids=cell_ids)


soft_near = 0.05
soft_far = 1.0


def pair_accel(target, sources):
    offset = sources[:, :3, None, :] - target[None, :3, :, None]
    dist_sq = jnp.sum(offset * offset, axis=1) + soft_near * soft_near
    weight = sources[:, 3, None, :] * dist_sq ** -1.5
    return jnp.sum(weight[:, None, :, :] * offset, axis=(0, 3))


def far_accel(position, centres, cell_mass):
    offset = centres[:, None, :] - position[:, :, None]
    dist_sq = jnp.sum(offset * offset, axis=0) + soft_far * soft_far
    weight = cell_mass[None, :] * dist_sq ** -1.5
    return jnp.sum(weight[None, :, :] * offset, axis=2)


def cell_centres(total, half_gy):
    cell = jnp.arange(total, dtype=jnp.int32)
    group = cell // SUBC
    sub_cell = cell % SUBC
    centre_x = (2 * (group // half_gy) + 1).astype(jnp.float32)
    centre_y = (2 * (group % half_gy) + 1).astype(jnp.float32)
    centre_z = (sub_cell.astype(jnp.float32) + 0.5) / SUBC
    return jnp.stack([centre_x, centre_y, centre_z], axis=0)


def reference(blocks, active_counts, pair_lists, cell_ids):
    total = (N_GX // 2) * (N_GY // 2) * SUBC
    block_mass = jnp.sum(blocks[:, :, :, 3, :], axis=-1)
    cell_mass = jax.ops.segment_sum(block_mass.reshape(-1), cell_ids.reshape(-1), num_segments=total)
    centres = cell_centres(total, N_GY // 2)

    def one_domain(device):
        row = device // N_GY
        col = device % N_GY
        pieces = []
        for step_a in range(3):
            for step_b in range(3):
                source = blocks[(row + step_a - 1) % N_GX, (col + step_b - 1) % N_GY]
                moved = jnp.array([step_a - 1, step_b - 1, 0, 0], dtype=jnp.float32)[:, None]
                pieces.append(source + moved)
        table = jnp.stack(pieces, axis=0).reshape(9 * NB, 4, BLOCK)
        local = blocks[row, col]
        corner = jnp.stack([row, col, 0]).astype(jnp.float32)[:, None]

        def one_slot(slot_index):
            target = local[slot_index]
            near = pair_accel(target, table[pair_lists[row, col, slot_index]])
            far = far_accel(target[:3] + corner, centres, cell_mass)
            return jnp.where(slot_index < active_counts[row, col], near + far, jnp.zeros_like(near))

        return lax.map(one_slot, jnp.arange(ACT, dtype=jnp.int32))

    result = lax.map(one_domain, jnp.arange(N_GX * N_GY, dtype=jnp.int32))
    return result.reshape(N_GX, N_GY, ACT, 3, BLOCK)
```

```python
import functools

import jax
import jax.numpy as jnp
from jax import lax
from jax.experimental import pallas as pl
from jax.experimental.pallas import tpu as pltpu
from jax.sharding import PartitionSpec as P

SUBC = 2
F32 = jnp.float32
BF16 = jnp.bfloat16

soft_near = 0.05
soft_far = 1.0
middle = 0.5


def swap(block, axis, odd):
    count = lax.axis_size(axis)
    pairs = []
    for low in range(odd, count, 2):
        high = (low + 1) % count
        pairs += [(low, high), (high, low)]
    return lax.ppermute(block, axis, pairs)


def total_over(values, axes):
    for axis in axes:
        count = lax.axis_size(axis)
        if count & (count - 1):
            values = lax.psum(values, axis)
            continue
        step = 1
        while step < count:
            values = values + lax.ppermute(values, axis, [(i, i ^ step) for i in range(count)])
            step *= 2
    return values


def split3(v):
    high = v.astype(BF16).astype(F32)
    rest = v - high
    mid = rest.astype(BF16).astype(F32)
    return high, mid, rest - mid


def source_rows(x, y, z):
    rows = []
    for v in (x, y, z):
        high, mid, low = split3(-2.0 * v)
        rows += [high, high, high, mid, mid, low]
    return rows + list(split3((x * x + y * y) + z * z))


def target_rows(x, y, z):
    rows = []
    for v in (x, y, z):
        high, mid, low = split3(v)
        rows += [high, mid, low, high, mid, high]
    one = jnp.ones_like(x)
    rows += [one, one, one]
    rows += list(split3(((x * x + y * y) + z * z) + soft_near * soft_near))
    return rows


def forces(place, limit, lists, cell_mass, *refs, count_blocks, half_gy):
    pieces, out = refs[:9], refs[9]
    table, picked, feature, moment, sems = refs[10:]
    slots, entries = lists.shape
    total = cell_mass.shape[0]
    rows = count_blocks * 4
    depth = feature.shape[1]
    even_x, even_y = place[2], place[3]

    copies = []
    for p in range(9):
        row, col = p // 3, p % 3
        a = (1, 2 * even_x, 2 - 2 * even_x)[row]
        b = (1, 2 * even_y, 2 - 2 * even_y)[col]
        at = pl.multiple_of((3 * a + b) * rows, rows)
        copy = pltpu.make_async_copy(pieces[p], table.at[pl.ds(at, rows), :], sems.at[p])
        copy.start()
        copies.append(copy)
    feature[:, 21:24, :] = jnp.ones_like(feature[:, 21:24, :])
    feature[:, 24:depth, :] = jnp.zeros_like(feature[:, 24:depth, :])
    moment[...] = jnp.zeros_like(moment)
    for copy in copies:
        copy.wait()

    line = lax.broadcasted_iota(jnp.int32, (rows, table.shape[1]), 0) % 4
    for a in range(3):
        for b in range(3):
            if (a, b) != (1, 1):
                at = (3 * a + b) * rows
                moved = jnp.where(line == 0, float(a - 1), jnp.where(line == 1, float(b - 1), 0.0))
                table[at : at + rows, :] = table[at : at + rows, :] + moved

    home = 4 * rows

    def one_slot(slot, carry):
        for k in range(entries):
            at = pl.multiple_of(lists[slot, k] * 4, 4)
            picked[4 * k : 4 * k + 4, :] = table[pl.ds(at, 4), :]
        x, y, z, mass = [picked[pl.ds(c, entries, stride=4), :] for c in range(4)]
        x, y, z = x - middle, y - middle, z - middle
        for i, row in enumerate(source_rows(x, y, z)):
            feature[:, i, :] = row
        for c, value in enumerate((mass * x, mass * y, mass * z, mass)):
            for p, part in enumerate(split3(value)):
                moment[:, 4 * p + c, :] = part
        target = table[pl.ds(pl.multiple_of(home + slot * 4, 4), 4), :]
        tx, ty, tz = [target[c : c + 1] - middle for c in range(3)]
        near = target_rows(tx, ty, tz)
        near += [jnp.zeros_like(tx)] * (depth - len(near))
        near = jnp.concatenate(near, axis=0).astype(BF16)
        sums = jnp.zeros((moment.shape[1], table.shape[1]), F32)
        for k in range(0, entries, 2):
            here = jnp.concatenate([feature[k], feature[k + 1]], axis=1).astype(BF16)
            dist_sq = lax.dot_general(here, near, (((0,), (0,)), ((), ())), preferred_element_type=F32)
            inverse = lax.rsqrt(dist_sq)
            weight = inverse * inverse * inverse
            parts = jnp.concatenate([moment[k], moment[k + 1]], axis=1).astype(BF16)
            high = weight.astype(BF16)
            low = (weight - high.astype(F32)).astype(BF16)
            sums += jnp.dot(parts, high, preferred_element_type=F32)
            sums += jnp.dot(parts, low, preferred_element_type=F32)
        sums = (sums[0:4] + sums[4:8]) + sums[8:12]
        for c, t in enumerate((tx, ty, tz)):
            out[slot, c : c + 1, :] = sums[c : c + 1] - t * sums[3:4]
        return carry

    lax.fori_loop(0, limit[0], one_slot, 0)

    corner = (place[0].astype(F32), place[1].astype(F32), 0.0)
    position = [table[pl.ds(home + c, slots, stride=4), :] + corner[c] for c in range(3)]

    def one_cell(cell, carry):
        group, sub_cell = cell // SUBC, cell % SUBC
        centre = (
            (2 * (group // half_gy) + 1).astype(F32),
            (2 * (group % half_gy) + 1).astype(F32),
            (sub_cell.astype(F32) + 0.5) * (1.0 / SUBC),
        )
        offset = [centre[c] - position[c] for c in range(3)]
        dist_sq = (offset[0] * offset[0] + offset[1] * offset[1]) + offset[2] * offset[2]
        inverse = lax.rsqrt(dist_sq + soft_far * soft_far)
        weight = cell_mass[cell] * (inverse * inverse * inverse)
        return tuple(carry[c] + weight * offset[c] for c in range(3))

    far = lax.fori_loop(0, total, one_cell, tuple(jnp.zeros_like(v) for v in position))
    active = lax.broadcasted_iota(jnp.int32, far[0].shape, 0) < limit[0]
    for c in range(3):
        out[:, c, :] = jnp.where(active, out[:, c, :] + far[c], 0.0)


def body(blocks, active_counts, pair_lists, cell_ids):
    count_blocks, width = blocks.shape[2], blocks.shape[4]
    slots, entries = pair_lists.shape[2:]
    half_gy = lax.axis_size("gy") // 2
    total = lax.axis_size("gx") // 2 * half_gy * SUBC
    own = blocks.reshape(count_blocks * 4, width)

    first_x = swap(own, "gx", 0)
    first_y = swap(own, "gy", 0)
    second_y = swap(own, "gy", 1)
    second_x = swap(own, "gx", 1)
    pieces = [own, first_y, second_y]
    for row in (first_x, second_x):
        pieces += [row, swap(row, "gy", 0), swap(row, "gy", 1)]

    block_mass = jnp.sum(blocks[0, 0, :, 3, :], axis=-1)
    member = cell_ids[0, 0][:, None] == jnp.arange(total, dtype=jnp.int32)[None, :]
    partial_mass = jnp.sum(jnp.where(member, block_mass[:, None], 0.0), axis=0)
    cell_mass = total_over(partial_mass, ("gx", "gy"))

    row, col = lax.axis_index("gx"), lax.axis_index("gy")
    place = jnp.stack([row, col, 1 - row % 2, 1 - col % 2]).astype(jnp.int32)
    smem = pl.BlockSpec(memory_space=pltpu.SMEM)
    result = pl.pallas_call(
        functools.partial(forces, count_blocks=count_blocks, half_gy=half_gy),
        out_shape=jax.ShapeDtypeStruct((slots, 3, width), F32),
        in_specs=[smem] * 4 + [pl.BlockSpec(memory_space=pl.ANY)] * 9,
        out_specs=pl.BlockSpec(memory_space=pltpu.VMEM),
        scratch_shapes=[
            pltpu.VMEM((9 * count_blocks * 4, width), F32),
            pltpu.VMEM((entries * 4, width), F32),
            pltpu.VMEM((entries, 32, width), F32),
            pltpu.VMEM((entries, 16, width), F32),
            pltpu.SemaphoreType.DMA((9,)),
        ],
        compiler_params=pltpu.CompilerParams(vmem_limit_bytes=16 * 2**20),
    )(place, active_counts.reshape(1), pair_lists[0, 0], cell_mass, *pieces)
    return result[None, None]


def solution(mesh):
    in_specs = (
        P("gx", "gy", None, None, None),
        P("gx", "gy"),
        P("gx", "gy", None, None),
        P("gx", "gy", None),
    )
    out_specs = P("gx", "gy", None, None, None)
    return jax.shard_map(body, mesh=mesh, in_specs=in_specs, out_specs=out_specs, check_vma=False)
```

```python
import functools
import math

import jax
import jax.numpy as jnp
from jax import lax
from jax.experimental import pallas as pl
from jax.experimental.pallas import tpu as pltpu
from jax.sharding import PartitionSpec as P

SUBC = 2
F32 = jnp.float32
BF16 = jnp.bfloat16

soft_near = 0.05
soft_far = 1.0
middle = 0.5


def swap(block, axis, odd):
    count = lax.axis_size(axis)
    pairs = []
    for low in range(odd, count, 2):
        high = (low + 1) % count
        pairs += [(low, high), (high, low)]
    return lax.ppermute(block, axis, pairs)


def total_over(values, axes):
    for axis in axes:
        count = lax.axis_size(axis)
        if count & (count - 1):
            values = lax.psum(values, axis)
            continue
        step = 1
        while step < count:
            values = values + lax.ppermute(values, axis, [(i, i ^ step) for i in range(count)])
            step *= 2
    return values


def split3(v):
    high = v.astype(BF16).astype(F32)
    rest = v - high
    mid = rest.astype(BF16).astype(F32)
    return high, mid, rest - mid


def roll(v, step):
    return pltpu.roll(v, step, 0)


def halves(low_half, pairs):
    upper = [jnp.where(low_half, first, roll(second, 4)) for first, second in pairs]
    lower = [jnp.where(low_half, roll(first, 4), second) for first, second in pairs]
    return [jnp.concatenate(rows, axis=0).astype(BF16) for rows in (upper, lower)]


def square_norm(is_mass, centred):
    square = jnp.where(is_mass, 0.0, centred)
    square = square * square
    return (roll(square, 1) + roll(square, 2)) + roll(square, 3)


def source_tile(tile, moved, is_mass, low_half):
    zero = jnp.zeros_like(tile)
    centred = (tile + moved) - jnp.where(is_mass, 0.0, middle)
    rows = jnp.where(is_mass, square_norm(is_mass, centred), -2.0 * centred)
    high, mid, low = split3(rows)
    high_1, mid_1 = jnp.where(is_mass, 1.0, high), jnp.where(is_mass, 1.0, mid)
    features = halves(low_half, [(high, high_1), (high_1, mid), (mid_1, low), (zero, zero)])
    mass = jnp.where(is_mass, tile, 0.0)
    mass = (mass + roll(mass, 7)) + (roll(mass, 6) + roll(mass, 5))
    high, mid, low = split3(jnp.where(is_mass, 1.0, centred) * mass)
    return features, halves(low_half, [(high, mid), (low, zero)])


def target_tile(tile, is_mass, low_half):
    zero = jnp.zeros_like(tile)
    centred = tile - middle
    norm = square_norm(is_mass, centred) + soft_near * soft_near
    high, mid, low = split3(jnp.where(is_mass, norm, centred))
    one_high = jnp.where(is_mass, 1.0, high)
    high_mid = jnp.where(is_mass, high, mid)
    mid_low = jnp.where(is_mass, mid, low)
    low_mid = jnp.where(is_mass, low, mid)
    return halves(low_half, [(one_high, high_mid), (mid_low, one_high), (low_mid, one_high), (zero, zero)])


def forces(place, limit, lists, cell_mass, *refs, count_blocks, half_gy, together):
    pieces, out = refs[:9], refs[9]
    table, feature, moment, target, sems = refs[10:]
    slots, entries = lists.shape
    width = table.shape[1]
    total = cell_mass.shape[0]
    rows = count_blocks * 4
    even_x, even_y = place[2], place[3]

    copies = []
    for p in range(9):
        row, col = p // 3, p % 3
        a = (1, 2 * even_x, 2 - 2 * even_x)[row]
        b = (1, 2 * even_y, 2 - 2 * even_y)[col]
        at = pl.multiple_of((3 * a + b) * rows, rows)
        copy = pltpu.make_async_copy(pieces[p], table.at[pl.ds(at, rows), :], sems.at[p])
        copy.start()
        copies.append(copy)
    for copy in copies:
        copy.wait()

    line = lax.broadcasted_iota(jnp.int32, (8, width), 0)
    is_mass, low_half = line % 4 == 3, line < 4
    is_x, is_y = line % 4 == 0, line % 4 == 1
    tiles = count_blocks // 2

    def one_domain(domain, carry):
        step_a = (domain // 3 - 1).astype(F32)
        step_b = (domain % 3 - 1).astype(F32)
        moved = jnp.where(is_x, step_a, jnp.where(is_y, step_b, 0.0))

        def two_tiles(pair, carry):
            for u in range(2):
                at = domain * tiles + pair * 2 + u
                tile = table[pl.ds(pl.multiple_of(at * 8, 8), 8), :]
                features, moments = source_tile(tile, moved, is_mass, low_half)
                for half in range(2):
                    feature[2 * at + half] = features[half]
                    moment[2 * at + half] = moments[half]
            return carry

        return lax.fori_loop(0, tiles // 2, two_tiles, carry)

    lax.fori_loop(0, 9, one_domain, 0)

    home = 4 * rows

    def one_target(pair, carry):
        tile = table[pl.ds(pl.multiple_of(home + pair * 8, 8), 8), :]
        for half, value in enumerate(target_tile(tile, is_mass, low_half)):
            target[2 * pair + half] = value
        return carry

    lax.fori_loop(0, slots // 2, one_target, 0)

    def some_slots(group, carry):
        for u in range(together):
            slot = group * together + u
            near = target[slot]
            sums = jnp.zeros((moment.shape[1], width), F32)
            for k in range(0, entries, 2):
                one, two = lists[slot, k], lists[slot, k + 1]
                here = jnp.concatenate([feature[one], feature[two]], axis=1)
                parts = jnp.concatenate([moment[one], moment[two]], axis=1)
                dist_sq = lax.dot_general(here, near, (((0,), (0,)), ((), ())), preferred_element_type=F32)
                inverse = lax.rsqrt(dist_sq)
                weight = inverse * inverse * inverse
                high = weight.astype(BF16)
                low = (weight - high.astype(F32)).astype(BF16)
                sums += jnp.dot(parts, high, preferred_element_type=F32)
                sums += jnp.dot(parts, low, preferred_element_type=F32)
            sums = (sums[0:4] + sums[4:8]) + sums[8:12]
            own = table[pl.ds(pl.multiple_of(home + slot * 4, 4), 4), :] - middle
            for c in range(3):
                out[slot, c : c + 1, :] = sums[c : c + 1] - own[c : c + 1] * sums[3:4]
        return carry

    lax.fori_loop(0, (limit[0] + together - 1) // together, some_slots, 0)

    corner = (place[0].astype(F32), place[1].astype(F32), 0.0)
    position = [table[pl.ds(home + c, slots, stride=4), :] + corner[c] for c in range(3)]

    def one_cell(cell, carry):
        group, sub_cell = cell // SUBC, cell % SUBC
        centre = (
            (2 * (group // half_gy) + 1).astype(F32),
            (2 * (group % half_gy) + 1).astype(F32),
            (sub_cell.astype(F32) + 0.5) * (1.0 / SUBC),
        )
        offset = [centre[c] - position[c] for c in range(3)]
        dist_sq = (offset[0] * offset[0] + offset[1] * offset[1]) + offset[2] * offset[2]
        inverse = lax.rsqrt(dist_sq + soft_far * soft_far)
        weight = cell_mass[cell] * (inverse * inverse * inverse)
        return tuple(carry[c] + weight * offset[c] for c in range(3))

    far = lax.fori_loop(0, total, one_cell, tuple(jnp.zeros_like(v) for v in position))
    active = lax.broadcasted_iota(jnp.int32, far[0].shape, 0) < limit[0]
    for c in range(3):
        out[:, c, :] = jnp.where(active, out[:, c, :] + far[c], 0.0)


def body(blocks, active_counts, pair_lists, cell_ids):
    count_blocks, width = blocks.shape[2], blocks.shape[4]
    slots, entries = pair_lists.shape[2:]
    half_gy = lax.axis_size("gy") // 2
    total = lax.axis_size("gx") // 2 * half_gy * SUBC
    own = blocks.reshape(count_blocks * 4, width)

    first_x = swap(own, "gx", 0)
    first_y = swap(own, "gy", 0)
    second_y = swap(own, "gy", 1)
    second_x = swap(own, "gx", 1)
    pieces = [own, first_y, second_y]
    for row in (first_x, second_x):
        pieces += [row, swap(row, "gy", 0), swap(row, "gy", 1)]

    block_mass = jnp.sum(blocks[0, 0, :, 3, :], axis=-1)
    member = cell_ids[0, 0][:, None] == jnp.arange(total, dtype=jnp.int32)[None, :]
    partial_mass = jnp.sum(jnp.where(member, block_mass[:, None], 0.0), axis=0)
    cell_mass = total_over(partial_mass, ("gx", "gy"))

    row, col = lax.axis_index("gx"), lax.axis_index("gy")
    place = jnp.stack([row, col, 1 - row % 2, 1 - col % 2]).astype(jnp.int32)
    smem = pl.BlockSpec(memory_space=pltpu.SMEM)
    result = pl.pallas_call(
        functools.partial(forces, count_blocks=count_blocks, half_gy=half_gy, together=math.gcd(slots, 8)),
        out_shape=jax.ShapeDtypeStruct((slots, 3, width), F32),
        in_specs=[smem] * 4 + [pl.BlockSpec(memory_space=pl.ANY)] * 9,
        out_specs=pl.BlockSpec(memory_space=pltpu.VMEM),
        scratch_shapes=[
            pltpu.VMEM((9 * count_blocks * 4, width), F32),
            pltpu.VMEM((9 * count_blocks, 32, width), BF16),
            pltpu.VMEM((9 * count_blocks, 16, width), BF16),
            pltpu.VMEM((slots, 32, width), BF16),
            pltpu.SemaphoreType.DMA((9,)),
        ],
        compiler_params=pltpu.CompilerParams(vmem_limit_bytes=24 * 2**20),
    )(place, active_counts.reshape(1), pair_lists[0, 0], cell_mass, *pieces)
    return result[None, None]


def solution(mesh):
    in_specs = (
        P("gx", "gy", None, None, None),
        P("gx", "gy"),
        P("gx", "gy", None, None),
        P("gx", "gy", None),
    )
    out_specs = P("gx", "gy", None, None, None)
    return jax.shard_map(body, mesh=mesh, in_specs=in_specs, out_specs=out_specs, check_vma=False)
```

```python
import functools
import math

import jax
import jax.numpy as jnp
from jax import lax
from jax.experimental import pallas as pl
from jax.experimental.pallas import tpu as pltpu
from jax.sharding import PartitionSpec as P

SUBC = 2
F32 = jnp.float32
BF16 = jnp.bfloat16

soft_near = 0.05
soft_far = 1.0
middle = 0.5


def swap(block, axis, odd):
    count = lax.axis_size(axis)
    pairs = []
    for low in range(odd, count, 2):
        high = (low + 1) % count
        pairs += [(low, high), (high, low)]
    return lax.ppermute(block, axis, pairs)


def exchange(values, axis, step):
    return lax.ppermute(values, axis, [(i, i ^ step) for i in range(lax.axis_size(axis))])


def total_over(parts, axis, step, after):
    after = list(after)
    while step < lax.axis_size(axis):
        values = parts[0] + parts[1]
        if after:
            values = lax.optimization_barrier((values, *after.pop(0)))[0]
        parts = (values, exchange(values, axis, step))
        step *= 2
    return parts


def row_total(own, first, second, after):
    if lax.axis_size("gy") != 4:
        return total_over((own, first), "gy", 2, ())
    second = lax.optimization_barrier((second, *after))[0]
    return (own + first) + second, exchange(second, "gy", 1)


def split3(v):
    high = v.astype(BF16).astype(F32)
    rest = v - high
    mid = rest.astype(BF16).astype(F32)
    return high, mid, rest - mid


def roll(v, step):
    return pltpu.roll(v, step, 0)


def halves(low_half, pairs):
    upper = [jnp.where(low_half, first, roll(second, 4)) for first, second in pairs]
    lower = [jnp.where(low_half, roll(first, 4), second) for first, second in pairs]
    return [jnp.concatenate(rows, axis=0).astype(BF16) for rows in (upper, lower)]


def square_norm(is_mass, centred):
    square = jnp.where(is_mass, 0.0, centred)
    square = square * square
    return (roll(square, 1) + roll(square, 2)) + roll(square, 3)


def source_tile(tile, moved, is_mass, low_half):
    zero = jnp.zeros_like(tile)
    centred = (tile + moved) - jnp.where(is_mass, 0.0, middle)
    rows = jnp.where(is_mass, square_norm(is_mass, centred), -2.0 * centred)
    high, mid, low = split3(rows)
    high_1, mid_1 = jnp.where(is_mass, 1.0, high), jnp.where(is_mass, 1.0, mid)
    features = halves(low_half, [(high, high_1), (high_1, mid), (mid_1, low), (zero, zero)])
    mass = jnp.where(is_mass, tile, 0.0)
    mass = (mass + roll(mass, 7)) + (roll(mass, 6) + roll(mass, 5))
    high, mid, low = split3(jnp.where(is_mass, 1.0, centred) * mass)
    return features, halves(low_half, [(high, mid), (low, zero)])


def target_tile(tile, is_mass, low_half):
    zero = jnp.zeros_like(tile)
    centred = tile - middle
    norm = square_norm(is_mass, centred) + soft_near * soft_near
    high, mid, low = split3(jnp.where(is_mass, norm, centred))
    one_high = jnp.where(is_mass, 1.0, high)
    high_mid = jnp.where(is_mass, high, mid)
    mid_low = jnp.where(is_mass, mid, low)
    low_mid = jnp.where(is_mass, low, mid)
    return halves(low_half, [(one_high, high_mid), (mid_low, one_high), (low_mid, one_high), (zero, zero)])


def mark(blocks, ids, out, *, half_gy):
    rows, width = blocks.shape
    first = (lax.axis_index("gx") // 2 * half_gy + lax.axis_index("gy") // 2) * SUBC
    count = ids.shape[1]
    line = lax.broadcasted_iota(jnp.int32, (8, count), 0)
    member = jnp.where(ids[...] - first == line, 1.0, 0.0)
    mass = blocks[pl.ds(3, count, stride=4), :]
    sums = jnp.dot(member, mass, preferred_element_type=F32, precision=lax.Precision.HIGHEST)
    sums = jnp.sum(sums, axis=1, keepdims=True)
    shape = (out.shape[0] - rows, width)
    cell = lax.broadcasted_iota(jnp.int32, shape, 0) * width + lax.broadcasted_iota(jnp.int32, shape, 1)
    values = jnp.zeros(shape, F32)
    for h in range(SUBC):
        values = jnp.where(cell == first + h, jnp.broadcast_to(sums[h : h + 1], shape), values)
    out[:rows, :] = blocks[...]
    out[rows:, :] = values


def near_forces(limit, lists_in, *refs, count_blocks, together):
    pieces, out = refs[:9], refs[9]
    table, feature, moment, target, lists, sems = refs[10:]
    entries, slots = lists.shape
    width = table.shape[1]
    rows = count_blocks * 4
    row, col = lax.axis_index("gx"), lax.axis_index("gy")
    even_x, even_y = 1 - row % 2, 1 - col % 2

    copies, domains = [], []
    for p in range(9):
        a = (1, 2 * even_x, 2 - 2 * even_x)[p // 3]
        b = (1, 2 * even_y, 2 - 2 * even_y)[p % 3]
        domains.append((a, b))
        at = pl.multiple_of((3 * a + b) * rows, rows)
        copies.append(
            pltpu.make_async_copy(pieces[p].at[pl.ds(0, rows), :], table.at[pl.ds(at, rows), :], sems.at[p])
        )
    copies.append(pltpu.make_async_copy(lists_in, lists, sems.at[9]))
    for copy in copies:
        copy.start()

    line = lax.broadcasted_iota(jnp.int32, (8, width), 0)
    is_mass, low_half = line % 4 == 3, line < 4
    is_x, is_y = line % 4 == 0, line % 4 == 1
    tiles = count_blocks // 2

    for p in range(9):
        copies[p].wait()
        a, b = domains[p]
        step_a = jnp.asarray(a - 1, F32)
        step_b = jnp.asarray(b - 1, F32)
        moved = jnp.where(is_x, step_a, jnp.where(is_y, step_b, 0.0))

        def two_tiles(pair, carry, base=(3 * a + b) * tiles, moved=moved):
            for u in range(2):
                at = base + pair * 2 + u
                tile = table[pl.ds(pl.multiple_of(at * 8, 8), 8), :]
                features, moments = source_tile(tile, moved, is_mass, low_half)
                for half in range(2):
                    feature[2 * at + half] = features[half]
                    moment[2 * at + half] = moments[half]
            return carry

        lax.fori_loop(0, tiles // 2, two_tiles, 0)
    copies[9].wait()

    home = 4 * rows

    def one_target(pair, carry):
        tile = table[pl.ds(pl.multiple_of(home + pair * 8, 8), 8), :]
        for half, value in enumerate(target_tile(tile, is_mass, low_half)):
            target[2 * pair + half] = value
        return carry

    lax.fori_loop(0, slots // 2, one_target, 0)

    for c, start in enumerate((row.astype(F32), col.astype(F32), 0.0)):
        out[3 + c] = table[pl.ds(home + c, slots, stride=4), :] + start

    def some_slots(group, carry):
        for u in range(together):
            slot = group * together + u
            near = target[slot]
            sums = jnp.zeros((moment.shape[1], width), F32)
            for k in range(0, entries, 2):
                one, two = lists[k, slot], lists[k + 1, slot]
                here = jnp.concatenate([feature[one], feature[two]], axis=1)
                parts = jnp.concatenate([moment[one], moment[two]], axis=1)
                dist_sq = lax.dot_general(here, near, (((0,), (0,)), ((), ())), preferred_element_type=F32)
                inverse = lax.rsqrt(dist_sq)
                weight = inverse * inverse * inverse
                high = weight.astype(BF16)
                low = (weight - high.astype(F32)).astype(BF16)
                sums += jnp.dot(parts, high, preferred_element_type=F32)
                sums += jnp.dot(parts, low, preferred_element_type=F32)
            sums = (sums[0:4] + sums[4:8]) + sums[8:12]
            own = table[pl.ds(pl.multiple_of(home + slot * 4, 4), 4), :] - middle
            for c in range(3):
                out[c, pl.ds(slot, 1), :] = sums[c : c + 1] - own[c : c + 1] * sums[3:4]
        return carry

    lax.fori_loop(0, (limit[0] + together - 1) // together, some_slots, 0)


def add_far(limit, some_mass, more_mass, near, out, *, half_gy, unroll):
    slots, width = out.shape[1:]
    total = some_mass.shape[0]
    position = [near[3 + c] for c in range(3)]

    def cells(step, carry):
        for u in range(unroll):
            cell = step * unroll + u
            group, sub_cell = cell // SUBC, cell % SUBC
            centre = (
                (2 * (group // half_gy) + 1).astype(F32),
                (2 * (group % half_gy) + 1).astype(F32),
                (sub_cell.astype(F32) + 0.5) * (1.0 / SUBC),
            )
            offset = [centre[c] - position[c] for c in range(3)]
            dist_sq = (offset[0] * offset[0] + offset[1] * offset[1]) + offset[2] * offset[2]
            inverse = lax.rsqrt(dist_sq + soft_far * soft_far)
            weight = (some_mass[cell] + more_mass[cell]) * (inverse * inverse * inverse)
            carry = tuple(carry[c] + weight * offset[c] for c in range(3))
        return carry

    far = lax.fori_loop(0, total // unroll, cells, tuple(jnp.zeros_like(v) for v in position))
    active = lax.broadcasted_iota(jnp.int32, (slots, width), 0) < limit[0]
    for c in range(3):
        out[c] = jnp.where(active, near[c] + far[c], 0.0)


def body(blocks, active_counts, pair_lists, cell_ids):
    count_blocks, width = blocks.shape[2], blocks.shape[4]
    slots, entries = pair_lists.shape[2:]
    half_gy = lax.axis_size("gy") // 2
    total = lax.axis_size("gx") // 2 * half_gy * SUBC
    own = blocks.reshape(count_blocks * 4, width)
    limit = active_counts.reshape(1)
    smem = pl.BlockSpec(memory_space=pltpu.SMEM)
    vmem = pl.BlockSpec(memory_space=pltpu.VMEM)

    lines = 8 * -(-total // (8 * width))
    marked = pl.pallas_call(
        functools.partial(mark, half_gy=half_gy),
        out_shape=jax.ShapeDtypeStruct((count_blocks * 4 + lines, width), F32),
        in_specs=[vmem, vmem],
        out_specs=vmem,
    )(own, cell_ids[0])

    first_x = swap(own, "gx", 0)
    second_x = swap(own, "gx", 1)
    second_y = swap(marked, "gy", 1)
    first_y = swap(marked, "gy", 0)
    pieces = [own, first_y, second_y]
    for row in (first_x, second_x):
        pieces += [row, swap(row, "gy", 0), swap(row, "gy", 1)]
    masses = [piece[-lines:].reshape(-1)[:total] for piece in (marked, first_y, second_y)]
    parts = row_total(*masses, (pieces[4],))
    parts = total_over(parts, "gx", 1, ((pieces[7],), (), ()))

    near = pl.pallas_call(
        functools.partial(near_forces, count_blocks=count_blocks, together=math.gcd(slots, 8)),
        out_shape=jax.ShapeDtypeStruct((6, slots, width), F32),
        in_specs=[smem] + [pl.BlockSpec(memory_space=pl.ANY)] * 10,
        out_specs=vmem,
        scratch_shapes=[
            pltpu.VMEM((9 * count_blocks * 4, width), F32),
            pltpu.VMEM((9 * count_blocks, 32, width), BF16),
            pltpu.VMEM((9 * count_blocks, 16, width), BF16),
            pltpu.VMEM((slots, 32, width), BF16),
            pltpu.SMEM((entries, slots), jnp.int32),
            pltpu.SemaphoreType.DMA((10,)),
        ],
        compiler_params=pltpu.CompilerParams(vmem_limit_bytes=24 * 2**20),
        cost_estimate=pl.CostEstimate(
            flops=20 * slots * entries * width * width,
            bytes_accessed=40 * count_blocks * 4 * width,
            transcendentals=slots * entries * width * width,
        ),
    )(limit, pair_lists[0, 0].T, *pieces)

    result = pl.pallas_call(
        functools.partial(add_far, half_gy=half_gy, unroll=math.gcd(total, 16)),
        out_shape=jax.ShapeDtypeStruct((3, slots, width), F32),
        in_specs=[smem] * 3 + [vmem],
        out_specs=vmem,
    )(limit, *parts, near)
    return result.transpose(1, 0, 2)[None, None]


def solution(mesh):
    in_specs = (
        P("gx", "gy", None, None, None),
        P("gx", "gy"),
        P("gx", "gy", None, None),
        P("gx", "gy", None),
    )
    out_specs = P("gx", "gy", None, None, None)
    return jax.shard_map(body, mesh=mesh, in_specs=in_specs, out_specs=out_specs, check_vma=False)
```

```python
import functools
import math

import jax
import jax.numpy as jnp
from jax import lax
from jax.experimental import pallas as pl
from jax.experimental.pallas import tpu as pltpu
from jax.sharding import PartitionSpec as P

SUBC = 2
F32 = jnp.float32
BF16 = jnp.bfloat16

soft_near = 0.05
soft_far = 1.0
middle = 0.5


def swap(block, axis, odd):
    count = lax.axis_size(axis)
    pairs = []
    for low in range(odd, count, 2):
        high = (low + 1) % count
        pairs += [(low, high), (high, low)]
    return lax.ppermute(block, axis, pairs)


def exchange(values, axis, step):
    return lax.ppermute(values, axis, [(i, i ^ step) for i in range(lax.axis_size(axis))])


def split_slots(slots, together):
    groups = slots // together
    cuts = [0, max(1, groups // 4), groups]
    return [(a * together, (b - a) * together) for a, b in zip(cuts, cuts[1:]) if b > a]


def near_cost(slots, entries, width):
    pairs = slots * entries * width * width
    return pl.CostEstimate(flops=20 * pairs, bytes_accessed=3 * slots * width * 4, transcendentals=pairs)


def split3(v):
    high = v.astype(BF16).astype(F32)
    rest = v - high
    mid = rest.astype(BF16).astype(F32)
    return high, mid, rest - mid


def roll(v, step):
    return pltpu.roll(v, step, 0)


def halves(low_half, pairs):
    upper = [jnp.where(low_half, first, roll(second, 4)) for first, second in pairs]
    lower = [jnp.where(low_half, roll(first, 4), second) for first, second in pairs]
    return [jnp.concatenate(rows, axis=0).astype(BF16) for rows in (upper, lower)]


def square_norm(is_mass, centred):
    square = jnp.where(is_mass, 0.0, centred)
    square = square * square
    return (roll(square, 1) + roll(square, 2)) + roll(square, 3)


def source_tile(tile, moved, is_mass, low_half):
    zero = jnp.zeros_like(tile)
    centred = (tile + moved) - jnp.where(is_mass, 0.0, middle)
    rows = jnp.where(is_mass, square_norm(is_mass, centred), -2.0 * centred)
    high, mid, low = split3(rows)
    high_1, mid_1 = jnp.where(is_mass, 1.0, high), jnp.where(is_mass, 1.0, mid)
    features = halves(low_half, [(high, high_1), (high_1, mid), (mid_1, low), (zero, zero)])
    mass = jnp.where(is_mass, tile, 0.0)
    mass = (mass + roll(mass, 7)) + (roll(mass, 6) + roll(mass, 5))
    high, mid, low = split3(jnp.where(is_mass, 1.0, centred) * mass)
    return features, halves(low_half, [(high, mid), (low, zero)])


def target_tile(tile, is_mass, low_half):
    zero = jnp.zeros_like(tile)
    centred = tile - middle
    norm = square_norm(is_mass, centred) + soft_near * soft_near
    high, mid, low = split3(jnp.where(is_mass, norm, centred))
    one_high = jnp.where(is_mass, 1.0, high)
    high_mid = jnp.where(is_mass, high, mid)
    mid_low = jnp.where(is_mass, mid, low)
    low_mid = jnp.where(is_mass, low, mid)
    return halves(low_half, [(one_high, high_mid), (mid_low, one_high), (low_mid, one_high), (zero, zero)])


def mark(blocks, ids, out, sem, *, half_gy):
    rows, width = blocks.shape
    copy = pltpu.make_async_copy(blocks, out.at[pl.ds(0, rows), :], sem)
    copy.start()
    copy.wait()
    first = (lax.axis_index("gx") // 2 * half_gy + lax.axis_index("gy") // 2) * SUBC
    sums = [[jnp.zeros((1, width), F32)] * 4 for _ in range(SUBC)]
    for block in range(ids.shape[1]):
        mass = out[4 * block + 3 : 4 * block + 4, :]
        cell = ids[0, block] - first
        for h in range(SUBC):
            sums[h][block % 4] += jnp.where(cell == h, mass, 0.0)
    shape = (out.shape[0] - rows, width)
    cell = lax.broadcasted_iota(jnp.int32, shape, 0) * width + lax.broadcasted_iota(jnp.int32, shape, 1)
    values = jnp.zeros(shape, F32)
    for h in range(SUBC):
        total = jnp.sum((sums[h][0] + sums[h][1]) + (sums[h][2] + sums[h][3]), axis=1, keepdims=True)
        values = jnp.where(cell == first + h, jnp.broadcast_to(total, shape), values)
    out[rows:, :] = values


def add_sources(pieces, places, feature, moment, count_blocks):
    width = feature.shape[2]
    even_x, even_y = 1 - lax.axis_index("gx") % 2, 1 - lax.axis_index("gy") % 2
    line = lax.broadcasted_iota(jnp.int32, (8, width), 0)
    is_mass, low_half = line % 4 == 3, line < 4
    is_x, is_y = line % 4 == 0, line % 4 == 1
    tiles = count_blocks // 2
    for piece, (row, col) in zip(pieces, places):
        a = (1, 2 * even_x, 2 - 2 * even_x)[row]
        b = (1, 2 * even_y, 2 - 2 * even_y)[col]
        step_a = jnp.asarray(a - 1, F32)
        step_b = jnp.asarray(b - 1, F32)
        moved = jnp.where(is_x, step_a, jnp.where(is_y, step_b, 0.0))

        def some_tiles(group, carry, piece=piece, base=(3 * a + b) * tiles, moved=moved):
            for u in range(2):
                at = group * 2 + u
                tile = piece[pl.ds(pl.multiple_of(at * 8, 8), 8), :]
                features, moments = source_tile(tile, moved, is_mass, low_half)
                for half in range(2):
                    feature[2 * (base + at) + half] = features[half]
                    moment[2 * (base + at) + half] = moments[half]
            return carry

        lax.fori_loop(0, tiles // 2, some_tiles, 0)


def start_rows(lists_in, *refs, places, count_blocks):
    pieces, (feature, moment, target, centre, masses, lists, sem) = refs[:-7], refs[-7:]
    copy = pltpu.make_async_copy(lists_in, lists, sem)
    copy.start()
    slots, width = centre.shape[1:]
    own, first_x = pieces[:2]
    line = lax.broadcasted_iota(jnp.int32, (8, width), 0)
    is_mass, low_half = line % 4 == 3, line < 4
    for row in range(masses.shape[0] // width):
        at = count_blocks * 4 + row
        masses[pl.ds(row * width, width)] = own[at, :] + first_x[at, :]

    def one_target(pair, carry):
        tile = own[pl.ds(pl.multiple_of(pair * 8, 8), 8), :]
        for half, value in enumerate(target_tile(tile, is_mass, low_half)):
            target[2 * pair + half] = value
        return carry

    lax.fori_loop(0, slots // 2, one_target, 0)
    for c in range(3):
        centre[c] = own[pl.ds(c, slots, stride=4), :] - middle
    add_sources(pieces, places, feature, moment, count_blocks)
    copy.wait()


def more_rows(feature_in, moment_in, *refs, places, count_blocks):
    pieces, (feature, moment) = refs[:-2], refs[-2:]
    add_sources(pieces, places, feature, moment, count_blocks)


def pair_sums(first, count, limit, lists, feature, moment, target, centre, out, together):
    entries = lists.shape[0]

    def some_slots(group, carry):
        for u in range(together):
            at = group * together + u
            slot = first + at
            near = target[slot]
            sums = jnp.zeros((moment.shape[1], moment.shape[2]), F32)
            for k in range(0, entries, 2):
                one, two = lists[k, slot], lists[k + 1, slot]
                here = jnp.concatenate([feature[one], feature[two]], axis=1)
                parts = jnp.concatenate([moment[one], moment[two]], axis=1)
                dist_sq = lax.dot_general(here, near, (((0,), (0,)), ((), ())), preferred_element_type=F32)
                inverse = lax.rsqrt(dist_sq)
                weight = inverse * inverse * inverse
                high = weight.astype(BF16)
                low = (weight - high.astype(F32)).astype(BF16)
                sums += jnp.dot(parts, high, preferred_element_type=F32)
                sums += jnp.dot(parts, low, preferred_element_type=F32)
            sums = (sums[0:4] + sums[4:8]) + sums[8:12]
            for c in range(3):
                own = centre[c, pl.ds(slot, 1), :]
                out[c, pl.ds(at, 1), :] = sums[c : c + 1] - own * sums[3:4]
        return carry

    groups = jnp.clip(limit[0] - first + together - 1, 0, count) // together
    lax.fori_loop(0, groups, some_slots, 0)


def near_forces(limit, lists_in, tie, feature_in, moment_in, target, centre, *refs, places, count_blocks, first, together):
    pieces, (out, feature, moment, lists, sem) = refs[:-5], refs[-5:]
    copy = pltpu.make_async_copy(lists_in, lists, sem)
    copy.start()
    add_sources(pieces, places, feature, moment, count_blocks)
    copy.wait()
    pair_sums(first, out.shape[1], limit, lists, feature, moment, target, centre, out, together)


def add_far(limit, some_mass, more_mass, centre_in, *refs, half_gy, total, unroll):
    nears, out, near, centre, masses, sems = refs[:-5], *refs[-5:]
    slots, width = out.shape[1:]
    copies = [
        pltpu.make_async_copy(some_mass, masses.at[0], sems.at[0]),
        pltpu.make_async_copy(more_mass, masses.at[1], sems.at[1]),
        pltpu.make_async_copy(centre_in, centre, sems.at[2]),
    ]
    at = 0
    for k, piece in enumerate(nears):
        count = piece.shape[1]
        copies.append(pltpu.make_async_copy(piece, near.at[:, pl.ds(at, count), :], sems.at[3 + k]))
        at += count
    for copy in copies:
        copy.start()
    for copy in copies:
        copy.wait()
    corner = (lax.axis_index("gx").astype(F32) + middle, lax.axis_index("gy").astype(F32) + middle, middle)
    position = [centre[c] + corner[c] for c in range(3)]

    def cells(step, carry):
        for u in range(unroll):
            cell = step * unroll + u
            group, sub_cell = cell // SUBC, cell % SUBC
            centre = (
                (2 * (group // half_gy) + 1).astype(F32),
                (2 * (group % half_gy) + 1).astype(F32),
                (sub_cell.astype(F32) + 0.5) * (1.0 / SUBC),
            )
            offset = [centre[c] - position[c] for c in range(3)]
            dist_sq = (offset[0] * offset[0] + offset[1] * offset[1]) + offset[2] * offset[2]
            inverse = lax.rsqrt(dist_sq + soft_far * soft_far)
            weight = (masses[0, cell] + masses[1, cell]) * (inverse * inverse * inverse)
            carry = tuple(carry[c] + weight * offset[c] for c in range(3))
        return carry

    far = lax.fori_loop(0, total // unroll, cells, tuple(jnp.zeros_like(v) for v in position))
    active = lax.broadcasted_iota(jnp.int32, (slots, width), 0) < limit[0]
    for c in range(3):
        out[c] = jnp.where(active, near[c] + far[c], 0.0)


def body(blocks, active_counts, pair_lists, cell_ids):
    count_blocks, width = blocks.shape[2], blocks.shape[4]
    slots, entries = pair_lists.shape[2:]
    half_gy = lax.axis_size("gy") // 2
    total = lax.axis_size("gx") // 2 * half_gy * SUBC
    own = blocks.reshape(count_blocks * 4, width)
    limit = active_counts.reshape(1)
    smem = pl.BlockSpec(memory_space=pltpu.SMEM)
    vmem = pl.BlockSpec(memory_space=pltpu.VMEM)

    lines = -(-total // width)
    rows = count_blocks * 4
    hbm = pl.BlockSpec(memory_space=pl.ANY)
    marked = pl.pallas_call(
        functools.partial(mark, half_gy=half_gy),
        out_shape=jax.ShapeDtypeStruct((rows + 8 * -(-lines // 8), width), F32),
        in_specs=[pl.BlockSpec(memory_space=pltpu.HBM), smem],
        out_specs=vmem,
        scratch_shapes=[pltpu.SemaphoreType.DMA],
        compiler_params=pltpu.CompilerParams(vmem_limit_bytes=2 * 2**20),
    )(own, cell_ids[0])

    second_y = swap(own, "gy", 1)
    first_y = swap(own, "gy", 0)
    first_x = swap(marked, "gx", 0)
    second_x = swap(lax.optimization_barrier((own, marked))[0], "gx", 1)
    first_xy = swap(first_x, "gy", 0)
    first_xyy = swap(first_x, "gy", 1)

    grant = pltpu.CompilerParams(vmem_limit_bytes=16 * 2**20)
    rows_of = dict(count_blocks=count_blocks)
    *table, masses, lists = pl.pallas_call(
        functools.partial(start_rows, places=[(0, 0), (1, 0), (0, 1), (0, 2)], **rows_of),
        out_shape=[
            jax.ShapeDtypeStruct((9 * count_blocks, 32, width), BF16),
            jax.ShapeDtypeStruct((9 * count_blocks, 16, width), BF16),
            jax.ShapeDtypeStruct((slots, 32, width), BF16),
            jax.ShapeDtypeStruct((3, slots, width), F32),
            jax.ShapeDtypeStruct((lines * width,), F32),
            jax.ShapeDtypeStruct((entries, slots), jnp.int32),
        ],
        in_specs=[hbm] + [vmem] * 4,
        out_specs=[vmem] * 6,
        scratch_shapes=[pltpu.SemaphoreType.DMA],
        compiler_params=grant,
        cost_estimate=pl.CostEstimate(flops=1, bytes_accessed=1, transcendentals=0),
    )(pair_lists[0, 0].T, marked, first_x, first_y, second_y)

    second_x = lax.optimization_barrier((second_x, masses))[0]
    second_xy = swap(second_x, "gy", 0)
    second_xyy = swap(second_x, "gy", 1)
    table[:2] = pl.pallas_call(
        functools.partial(more_rows, places=[(1, 1), (2, 0), (2, 1)], **rows_of),
        out_shape=table[:2],
        in_specs=[vmem] * 5,
        out_specs=[vmem] * 2,
        input_output_aliases={0: 0, 1: 1},
        compiler_params=grant,
        cost_estimate=pl.CostEstimate(flops=1, bytes_accessed=1, transcendentals=0),
    )(*table[:2], first_xy, second_x, second_xy)
    late, late_places = [first_xyy, second_xyy], [(1, 2), (2, 2)]

    together = math.gcd(slots, 8)
    ranges = split_slots(slots, together)

    def near_part(k, tie, table):
        first, count = ranges[k]
        pieces, places = (late, late_places) if k == 0 else ([], [])
        near, *rows = pl.pallas_call(
            functools.partial(near_forces, places=places, count_blocks=count_blocks, first=first, together=together),
            out_shape=[jax.ShapeDtypeStruct((3, count, width), F32), *table[:2]],
            in_specs=[smem] + [hbm] * 2 + [vmem] * (4 + len(pieces)),
            out_specs=[vmem] * 3,
            scratch_shapes=[pltpu.SMEM((entries, slots), jnp.int32), pltpu.SemaphoreType.DMA],
            input_output_aliases={3: 1, 4: 2},
            compiler_params=pltpu.CompilerParams(vmem_limit_bytes=24 * 2**20),
            cost_estimate=near_cost(count, entries, width),
        )(limit, lists, tie, *table, *pieces)
        return near, [*rows, *table[2:]]

    values, nears = masses, []
    steps = [("gx", 2 << k) for k in range((lax.axis_size("gx") // 2).bit_length() - 1)]
    steps += [("gy", 1 << k) for k in range(lax.axis_size("gy").bit_length() - 1)]
    for k, (axis, step) in enumerate(steps):
        left = len(steps) - k
        if left == 3:
            values = lax.optimization_barrier((values, table[0], *late))[0]
        if left == 2 and nears:
            values = lax.optimization_barrier((values, nears[0]))[0]
        other = exchange(values, axis, step)
        if left in (1, 3) and len(nears) < len(ranges):
            near, table = near_part(len(nears), values, table)
            nears.append(near)
        parts = (values, other)
        values = values + other

    result = pl.pallas_call(
        functools.partial(add_far, half_gy=half_gy, total=total, unroll=math.gcd(total, 16)),
        out_shape=jax.ShapeDtypeStruct((3, slots, width), F32),
        in_specs=[smem] + [pl.BlockSpec(memory_space=pl.ANY)] * (3 + len(nears)),
        out_specs=vmem,
        scratch_shapes=[
            pltpu.VMEM((3, slots, width), F32),
            pltpu.VMEM((3, slots, width), F32),
            pltpu.SMEM((2, lines * width), F32),
            pltpu.SemaphoreType.DMA((3 + len(nears),)),
        ],
        compiler_params=pltpu.CompilerParams(vmem_limit_bytes=4 * 2**20),
    )(limit, *parts, table[3], *nears)
    return result.transpose(1, 0, 2)[None, None]


def solution(mesh):
    in_specs = (
        P("gx", "gy", None, None, None),
        P("gx", "gy"),
        P("gx", "gy", None, None),
        P("gx", "gy", None),
    )
    out_specs = P("gx", "gy", None, None, None)
    return jax.shard_map(body, mesh=mesh, in_specs=in_specs, out_specs=out_specs, check_vma=False)
```

```python
import functools
import math

import jax
import jax.numpy as jnp
from jax import lax
from jax.experimental import pallas as pl
from jax.experimental.pallas import tpu as pltpu
from jax.sharding import PartitionSpec as P

SUBC = 2
F32 = jnp.float32
BF16 = jnp.bfloat16

soft_near = 0.05
soft_far = 1.0
middle = 0.5


def swap(block, axis, odd):
    count = lax.axis_size(axis)
    pairs = []
    for low in range(odd, count, 2):
        high = (low + 1) % count
        pairs += [(low, high), (high, low)]
    return lax.ppermute(block, axis, pairs)


def exchange(values, axis, step):
    return lax.ppermute(values, axis, [(i, i ^ step) for i in range(lax.axis_size(axis))])


def split_slots(slots, together):
    groups = slots // together
    cuts = [0, max(1, groups // 4), groups]
    return [(a * together, (b - a) * together) for a, b in zip(cuts, cuts[1:]) if b > a]


def near_cost(slots, entries, width):
    pairs = slots * entries * width * width
    return pl.CostEstimate(flops=20 * pairs, bytes_accessed=3 * slots * width * 4, transcendentals=pairs)


def split3(v):
    high = v.astype(BF16).astype(F32)
    rest = v - high
    mid = rest.astype(BF16).astype(F32)
    return high, mid, rest - mid


def roll(v, step):
    return pltpu.roll(v, step, 0)


def halves(low_half, pairs):
    upper = [jnp.where(low_half, first, roll(second, 4)) for first, second in pairs]
    lower = [jnp.where(low_half, roll(first, 4), second) for first, second in pairs]
    return [jnp.concatenate(rows, axis=0).astype(BF16) for rows in (upper, lower)]


def square_norm(is_mass, centred):
    square = jnp.where(is_mass, 0.0, centred)
    square = square * square
    return (roll(square, 1) + roll(square, 2)) + roll(square, 3)


def source_tile(tile, moved, is_mass, low_half):
    zero = jnp.zeros_like(tile)
    centred = (tile + moved) - jnp.where(is_mass, 0.0, middle)
    rows = jnp.where(is_mass, square_norm(is_mass, centred), -2.0 * centred)
    high, mid, low = split3(rows)
    high_1, mid_1 = jnp.where(is_mass, 1.0, high), jnp.where(is_mass, 1.0, mid)
    features = halves(low_half, [(high, high_1), (high_1, mid), (mid_1, low), (zero, zero)])
    mass = jnp.where(is_mass, tile, 0.0)
    mass = (mass + roll(mass, 7)) + (roll(mass, 6) + roll(mass, 5))
    high, mid, low = split3(jnp.where(is_mass, 1.0, centred) * mass)
    return features, halves(low_half, [(high, mid), (low, zero)])


def target_tile(tile, is_mass, low_half):
    zero = jnp.zeros_like(tile)
    centred = tile - middle
    norm = square_norm(is_mass, centred) + soft_near * soft_near
    high, mid, low = split3(jnp.where(is_mass, norm, centred))
    one_high = jnp.where(is_mass, 1.0, high)
    high_mid = jnp.where(is_mass, high, mid)
    mid_low = jnp.where(is_mass, mid, low)
    low_mid = jnp.where(is_mass, low, mid)
    return halves(low_half, [(one_high, high_mid), (mid_low, one_high), (low_mid, one_high), (zero, zero)])


def mark(blocks, ids_in, out, ids, sems, *, half_gy):
    rows, width = blocks.shape
    copies = [
        pltpu.make_async_copy(ids_in, ids, sems.at[0]),
        pltpu.make_async_copy(blocks, out.at[pl.ds(0, rows), :], sems.at[1]),
    ]
    for copy in copies:
        copy.start()
    for copy in copies:
        copy.wait()
    first = (lax.axis_index("gx") // 2 * half_gy + lax.axis_index("gy") // 2) * SUBC
    count = ids.shape[1]
    line = lax.broadcasted_iota(jnp.int32, (8, count), 0)
    member = jnp.where(ids[...] - first == line, 1.0, 0.0)
    mass = out[pl.ds(3, count, stride=4), :]
    sums = jnp.dot(member, mass, preferred_element_type=F32, precision=lax.Precision.HIGHEST)
    sums = jnp.sum(sums, axis=1, keepdims=True)
    shape = (out.shape[0] - rows, width)
    cell = lax.broadcasted_iota(jnp.int32, shape, 0) * width + lax.broadcasted_iota(jnp.int32, shape, 1)
    values = jnp.zeros(shape, F32)
    for h in range(SUBC):
        values = jnp.where(cell == first + h, jnp.broadcast_to(sums[h : h + 1], shape), values)
    out[rows:, :] = values


def add_sources(pieces, places, feature, moment, count_blocks):
    width = feature.shape[2]
    even_x, even_y = 1 - lax.axis_index("gx") % 2, 1 - lax.axis_index("gy") % 2
    line = lax.broadcasted_iota(jnp.int32, (8, width), 0)
    is_mass, low_half = line % 4 == 3, line < 4
    is_x, is_y = line % 4 == 0, line % 4 == 1
    tiles = count_blocks // 2
    for piece, (row, col) in zip(pieces, places):
        a = (1, 2 * even_x, 2 - 2 * even_x)[row]
        b = (1, 2 * even_y, 2 - 2 * even_y)[col]
        step_a = jnp.asarray(a - 1, F32)
        step_b = jnp.asarray(b - 1, F32)
        moved = jnp.where(is_x, step_a, jnp.where(is_y, step_b, 0.0))

        def some_tiles(group, carry, piece=piece, base=(3 * a + b) * tiles, moved=moved):
            for u in range(2):
                at = group * 2 + u
                tile = piece[pl.ds(pl.multiple_of(at * 8, 8), 8), :]
                features, moments = source_tile(tile, moved, is_mass, low_half)
                for half in range(2):
                    feature[2 * (base + at) + half] = features[half]
                    moment[2 * (base + at) + half] = moments[half]
            return carry

        lax.fori_loop(0, tiles // 2, some_tiles, 0)


def start_rows(*refs, places, count_blocks):
    pieces, (feature, moment, target, centre) = refs[:-4], refs[-4:]
    slots, width = centre.shape[1:]
    own = pieces[0]
    line = lax.broadcasted_iota(jnp.int32, (8, width), 0)
    is_mass, low_half = line % 4 == 3, line < 4

    def one_target(pair, carry):
        tile = own[pl.ds(pl.multiple_of(pair * 8, 8), 8), :]
        for half, value in enumerate(target_tile(tile, is_mass, low_half)):
            target[2 * pair + half] = value
        return carry

    lax.fori_loop(0, slots // 2, one_target, 0)
    for c in range(3):
        centre[c] = own[pl.ds(c, slots, stride=4), :] - middle
    add_sources(pieces, places, feature, moment, count_blocks)


def more_rows(feature_in, moment_in, *refs, places, count_blocks):
    pieces, (feature, moment) = refs[:-2], refs[-2:]
    add_sources(pieces, places, feature, moment, count_blocks)


def last_rows(feature_in, moment_in, *refs, places, count_blocks, here, there):
    pieces, (feature, moment, here_mass, there_mass) = refs[:-4], refs[-4:]
    width = feature.shape[2]
    for row in range(here_mass.shape[0] // width):
        for out, members in ((here_mass, here), (there_mass, there)):
            values = [pieces[k][count_blocks * 4 + row, :] for k in members]
            out[pl.ds(row * width, width)] = functools.reduce(jnp.add, values)
    add_sources(pieces[: len(places)], places, feature, moment, count_blocks)


def pair_sums(first, count, limit, lists, feature, moment, target, centre, out, together):
    entries = lists.shape[0]

    def some_slots(group, carry):
        for u in range(together):
            at = group * together + u
            slot = first + at
            near = target[slot]
            sums = jnp.zeros((moment.shape[1], moment.shape[2]), F32)
            for k in range(0, entries, 2):
                one, two = lists[k, slot], lists[k + 1, slot]
                here = jnp.concatenate([feature[one], feature[two]], axis=1)
                parts = jnp.concatenate([moment[one], moment[two]], axis=1)
                dist_sq = lax.dot_general(here, near, (((0,), (0,)), ((), ())), preferred_element_type=F32)
                inverse = lax.rsqrt(dist_sq)
                weight = inverse * inverse * inverse
                high = weight.astype(BF16)
                low = (weight - high.astype(F32)).astype(BF16)
                sums += jnp.dot(parts, high, preferred_element_type=F32)
                sums += jnp.dot(parts, low, preferred_element_type=F32)
            sums = (sums[0:4] + sums[4:8]) + sums[8:12]
            for c in range(3):
                own = centre[c, pl.ds(slot, 1), :]
                out[c, pl.ds(at, 1), :] = sums[c : c + 1] - own * sums[3:4]
        return carry

    groups = jnp.clip(limit[0, 0] - first + together - 1, 0, count) // together
    lax.fori_loop(0, groups, some_slots, 0)


def near_forces(limit_in, lists_in, tie, feature_in, moment_in, target, centre, *refs, places, count_blocks, first, together):
    pieces, (out, feature, moment, lists, limit, sems) = refs[:-6], refs[-6:]
    copies = [pltpu.make_async_copy(lists_in, lists, sems.at[0]), pltpu.make_async_copy(limit_in, limit, sems.at[1])]
    for copy in copies:
        copy.start()
    add_sources(pieces, places, feature, moment, count_blocks)
    for copy in copies:
        copy.wait()
    pair_sums(first, out.shape[1], limit, lists, feature, moment, target, centre, out, together)


def add_far(limit_in, some_mass, more_mass, centre_in, *refs, half_gy, total, unroll):
    nears, out, near, centre, masses, limit, sems = refs[:-6], *refs[-6:]
    slots, width = out.shape[1:]
    copies = [
        pltpu.make_async_copy(some_mass, masses.at[0], sems.at[0]),
        pltpu.make_async_copy(more_mass, masses.at[1], sems.at[1]),
        pltpu.make_async_copy(centre_in, centre, sems.at[2]),
        pltpu.make_async_copy(limit_in, limit, sems.at[3]),
    ]
    at = 0
    for k, piece in enumerate(nears):
        count = piece.shape[1]
        copies.append(pltpu.make_async_copy(piece, near.at[:, pl.ds(at, count), :], sems.at[4 + k]))
        at += count
    for copy in copies:
        copy.start()
    for copy in copies:
        copy.wait()
    corner = (lax.axis_index("gx").astype(F32) + middle, lax.axis_index("gy").astype(F32) + middle, middle)
    position = [centre[c] + corner[c] for c in range(3)]

    def cells(step, carry):
        for u in range(unroll):
            cell = step * unroll + u
            group, sub_cell = cell // SUBC, cell % SUBC
            centre = (
                (2 * (group // half_gy) + 1).astype(F32),
                (2 * (group % half_gy) + 1).astype(F32),
                (sub_cell.astype(F32) + 0.5) * (1.0 / SUBC),
            )
            offset = [centre[c] - position[c] for c in range(3)]
            dist_sq = (offset[0] * offset[0] + offset[1] * offset[1]) + offset[2] * offset[2]
            inverse = lax.rsqrt(dist_sq + soft_far * soft_far)
            weight = (masses[0, cell] + masses[1, cell]) * (inverse * inverse * inverse)
            carry = tuple(carry[c] + weight * offset[c] for c in range(3))
        return carry

    far = lax.fori_loop(0, total // unroll, cells, tuple(jnp.zeros_like(v) for v in position))
    active = lax.broadcasted_iota(jnp.int32, (slots, width), 0) < limit[0, 0]
    for c in range(3):
        out[c] = jnp.where(active, near[c] + far[c], 0.0)


def body(blocks, active_counts, pair_lists, cell_ids):
    count_blocks, width = blocks.shape[2], blocks.shape[4]
    slots, entries = pair_lists.shape[2:]
    half_gy = lax.axis_size("gy") // 2
    total = lax.axis_size("gx") // 2 * half_gy * SUBC
    own = blocks.reshape(count_blocks * 4, width)
    smem = pl.BlockSpec(memory_space=pltpu.SMEM)
    vmem = pl.BlockSpec(memory_space=pltpu.VMEM)

    lines = -(-total // width)
    rows = count_blocks * 4
    hbm = pl.BlockSpec(memory_space=pl.ANY)
    marked = pl.pallas_call(
        functools.partial(mark, half_gy=half_gy),
        out_shape=jax.ShapeDtypeStruct((rows + 8 * -(-lines // 8), width), F32),
        in_specs=[hbm] * 2,
        out_specs=vmem,
        scratch_shapes=[pltpu.VMEM((1, count_blocks), jnp.int32), pltpu.SemaphoreType.DMA((2,))],
        compiler_params=pltpu.CompilerParams(vmem_limit_bytes=2 * 2**20),
    )(own, cell_ids[0])
    lists = pair_lists[0, 0].T

    first_x = swap(marked, "gx", 0)
    second_y = swap(marked, "gy", 1)
    first_y = swap(marked, "gy", 0)
    second_x = swap(lax.optimization_barrier((own, marked))[0], "gx", 1)
    row_params = dict(
        compiler_params=pltpu.CompilerParams(vmem_limit_bytes=16 * 2**20),
        cost_estimate=pl.CostEstimate(flops=1, bytes_accessed=1, transcendentals=0),
    )
    table = list(pl.pallas_call(
        functools.partial(start_rows, places=[(0, 0)], count_blocks=count_blocks),
        out_shape=[
            jax.ShapeDtypeStruct((9 * count_blocks, 32, width), BF16),
            jax.ShapeDtypeStruct((9 * count_blocks, 16, width), BF16),
            jax.ShapeDtypeStruct((slots, 32, width), BF16),
            jax.ShapeDtypeStruct((3, slots, width), F32),
        ],
        in_specs=[vmem],
        out_specs=[vmem] * 4,
        **row_params,
    )(marked))

    second_x = second_x
    first_x = lax.optimization_barrier((first_x, table[3]))[0]
    first_xy = swap(first_x, "gy", 0)
    first_xyy = swap(first_x, "gy", 1)

    table[:2] = pl.pallas_call(
        functools.partial(more_rows, places=[(1, 0), (0, 1), (0, 2)], count_blocks=count_blocks),
        out_shape=table[:2],
        in_specs=[vmem] * 5,
        out_specs=[vmem] * 2,
        input_output_aliases={0: 0, 1: 1},
        **row_params,
    )(*table[:2], first_x, first_y, second_y)

    second_xy = swap(second_x, "gy", 0)
    second_xyy = swap(second_x, "gy", 1)
    more = [first_xy, second_x, second_xy, first_xyy, marked, first_x, first_y, second_y]
    *rows_now, here_mass, there_mass = pl.pallas_call(
        functools.partial(
            last_rows,
            places=[(1, 1), (2, 0), (2, 1), (1, 2)],
            count_blocks=count_blocks,
            here=(0, 4, 5, 6),
            there=(3, 7),
        ),
        out_shape=[*table[:2]] + [jax.ShapeDtypeStruct((lines * width,), F32)] * 2,
        in_specs=[vmem] * (2 + len(more)),
        out_specs=[vmem] * 4,
        input_output_aliases={0: 0, 1: 1},
        **row_params,
    )(*table[:2], *more)
    table = [*rows_now, *table[2:]]
    late, late_places = [second_xyy], [(2, 2)]

    together = math.gcd(slots, 8)
    ranges = split_slots(slots, together)

    def near_part(k, tie, table):
        first, count = ranges[k]
        pieces, places = (late, late_places) if k == 0 else ([], [])
        near, *rows = pl.pallas_call(
            functools.partial(
                near_forces, places=places, count_blocks=count_blocks, first=first, together=math.gcd(count, 12 if count % 12 == 0 else 8)
            ),
            out_shape=[jax.ShapeDtypeStruct((3, count, width), F32), *table[:2]],
            in_specs=[hbm] * 3 + [vmem] * (4 + len(pieces)),
            out_specs=[vmem] * 3,
            scratch_shapes=[
                pltpu.SMEM((entries, slots), jnp.int32),
                pltpu.SMEM((1, 1), jnp.int32),
                pltpu.SemaphoreType.DMA((2,)),
            ],
            input_output_aliases={3: 1, 4: 2},
            compiler_params=pltpu.CompilerParams(vmem_limit_bytes=24 * 2**20),
            cost_estimate=near_cost(count, entries, width),
        )(active_counts, lists, tie, *table, *pieces)
        return near, [*rows, *table[2:]]

    if lax.axis_size("gy") == 4:
        there_mass = lax.optimization_barrier((there_mass, second_xyy))[0]
        values = (here_mass + there_mass) + exchange(there_mass, "gy", 1)
        steps = []
    else:
        values = here_mass
        steps = [("gy", 2 << k) for k in range((lax.axis_size("gy") // 2).bit_length() - 1)]
    steps += [("gx", 2 << k) for k in range((lax.axis_size("gx") // 2).bit_length() - 1)]
    nears, parts = [], (values, jnp.zeros_like(values))
    for k, (axis, step) in enumerate(steps):
        if nears:
            values = lax.optimization_barrier((values, nears[-1]))[0]
        other = exchange(values, axis, step)
        parts = (values, other)
        if k >= len(steps) - 2 and len(nears) < len(ranges):
            near, table = near_part(len(nears), values, table)
            nears.append(near)
        values = values + other
    while len(nears) < len(ranges):
        near, table = near_part(len(nears), parts[0], table)
        nears.append(near)

    result = pl.pallas_call(
        functools.partial(add_far, half_gy=half_gy, total=total, unroll=math.gcd(total, 16)),
        out_shape=jax.ShapeDtypeStruct((3, slots, width), F32),
        in_specs=[hbm] * (4 + len(nears)),
        out_specs=vmem,
        scratch_shapes=[
            pltpu.VMEM((3, slots, width), F32),
            pltpu.VMEM((3, slots, width), F32),
            pltpu.SMEM((2, lines * width), F32),
            pltpu.SMEM((1, 1), jnp.int32),
            pltpu.SemaphoreType.DMA((4 + len(nears),)),
        ],
        compiler_params=pltpu.CompilerParams(vmem_limit_bytes=4 * 2**20),
    )(active_counts, *parts, table[3], *nears)
    return result.transpose(1, 0, 2)[None, None]


def solution(mesh):
    in_specs = (
        P("gx", "gy", None, None, None),
        P("gx", "gy"),
        P("gx", "gy", None, None),
        P("gx", "gy", None),
    )
    out_specs = P("gx", "gy", None, None, None)
    return jax.shard_map(body, mesh=mesh, in_specs=in_specs, out_specs=out_specs, check_vma=False)
```

```python
import functools
import math

import jax
import jax.numpy as jnp
from jax import lax
from jax.experimental import pallas as pl
from jax.experimental.pallas import tpu as pltpu
from jax.sharding import PartitionSpec as P

SUBC = 2
F32 = jnp.float32
BF16 = jnp.bfloat16

soft_near = 0.05
soft_far = 1.0
middle = 0.5


def swap(block, axis, odd):
    count = lax.axis_size(axis)
    pairs = []
    for low in range(odd, count, 2):
        high = (low + 1) % count
        pairs += [(low, high), (high, low)]
    return lax.ppermute(block, axis, pairs)


def exchange(values, axis, step):
    return lax.ppermute(values, axis, [(i, i ^ step) for i in range(lax.axis_size(axis))])


def split_slots(slots, together):
    groups = slots // together
    cuts = [0, max(1, groups // 4), groups]
    return [(a * together, (b - a) * together) for a, b in zip(cuts, cuts[1:]) if b > a]


def near_cost(slots, entries, width):
    pairs = slots * entries * width * width
    return pl.CostEstimate(flops=20 * pairs, bytes_accessed=3 * slots * width * 4, transcendentals=pairs)


def split3(v):
    high = v.astype(BF16).astype(F32)
    rest = v - high
    mid = rest.astype(BF16).astype(F32)
    return high, mid, rest - mid


def roll(v, step):
    return pltpu.roll(v, step, 0)


def halves(low_half, pairs):
    upper, lower = [], []
    for (first, first_rolled), second in pairs:
        second, second_rolled = second or (jnp.zeros_like(first),) * 2
        upper.append(jnp.where(low_half, first, second_rolled))
        lower.append(jnp.where(low_half, first_rolled, second))
    return upper, lower


def rows16(tiles):
    return jnp.concatenate(tiles, axis=0).astype(BF16)


def with_rolled(v):
    return v, roll(v, 4)


def masked(is_mass, value, pair):
    return tuple(jnp.where(is_mass, value, v) for v in pair)


def square_norm(is_mass, centred):
    square = jnp.where(is_mass, 0.0, centred)
    square = square * square
    square = square + roll(square, 1)
    return square + roll(square, 2)


def source_tile(tile, moved, is_mass, low_half):
    centred = (tile + moved) - jnp.where(is_mass, 0.0, middle)
    rows = jnp.where(is_mass, square_norm(is_mass, centred), -2.0 * centred)
    high, mid, low = map(with_rolled, split3(rows))
    high_1, mid_1 = masked(is_mass, 1.0, high), masked(is_mass, 1.0, mid)
    features = halves(low_half, [(high, high_1), (high_1, mid), (mid_1, low)])
    zero = jnp.zeros_like(tile)
    mass = jnp.where(is_mass, tile, 0.0)
    mass = mass + roll(mass, 7)
    mass = mass + roll(mass, 6)
    high, mid, low = map(with_rolled, split3(jnp.where(is_mass, 1.0, centred) * mass))
    moments = halves(low_half, [(high, mid), (low, None)])
    return [rows16([*v, zero]) for v in features], [rows16(v) for v in moments]


def target_tile(tile, is_mass, low_half):
    centred = tile - middle
    norm = square_norm(is_mass, centred) + soft_near * soft_near
    high, mid, low = map(with_rolled, split3(jnp.where(is_mass, norm, centred)))
    one_high = masked(is_mass, 1.0, high)
    high_mid = tuple(jnp.where(is_mass, a, b) for a, b in zip(high, mid))
    mid_low = tuple(jnp.where(is_mass, a, b) for a, b in zip(mid, low))
    low_mid = tuple(jnp.where(is_mass, a, b) for a, b in zip(low, mid))
    groups = halves(low_half, [(one_high, high_mid), (mid_low, one_high), (low_mid, one_high)])
    return [rows16([*v, jnp.zeros_like(tile)]) for v in groups]


def mark(blocks, ids_in, out, ids, sems, *, half_gy):
    rows, width = blocks.shape
    copies = [
        pltpu.make_async_copy(ids_in, ids, sems.at[0]),
        pltpu.make_async_copy(blocks, out.at[pl.ds(0, rows), :], sems.at[1]),
    ]
    for copy in copies:
        copy.start()
    for copy in copies:
        copy.wait()
    first = (lax.axis_index("gx") // 2 * half_gy + lax.axis_index("gy") // 2) * SUBC
    count = ids.shape[1]
    line = lax.broadcasted_iota(jnp.int32, (8, count), 0)
    member = jnp.where(ids[...] - first == line, 1.0, 0.0)
    mass = out[pl.ds(3, count, stride=4), :]
    sums = jnp.dot(member, mass, preferred_element_type=F32, precision=lax.Precision.HIGHEST)
    sums = jnp.sum(sums, axis=1, keepdims=True)
    shape = (out.shape[0] - rows, width)
    cell = lax.broadcasted_iota(jnp.int32, shape, 0) * width + lax.broadcasted_iota(jnp.int32, shape, 1)
    values = jnp.zeros(shape, F32)
    for h in range(SUBC):
        values = jnp.where(cell == first + h, jnp.broadcast_to(sums[h : h + 1], shape), values)
    out[rows:, :] = values


def add_sources(pieces, places, feature, moment, count_blocks):
    width = feature.shape[2]
    even_x, even_y = 1 - lax.axis_index("gx") % 2, 1 - lax.axis_index("gy") % 2
    line = lax.broadcasted_iota(jnp.int32, (8, width), 0)
    is_mass, low_half = line % 4 == 3, line < 4
    is_x, is_y = line % 4 == 0, line % 4 == 1
    tiles = count_blocks // 2
    unroll = math.gcd(tiles, 8)
    for piece, (row, col) in zip(pieces, places):
        a = (1, 2 * even_x, 2 - 2 * even_x)[row]
        b = (1, 2 * even_y, 2 - 2 * even_y)[col]
        step_a = jnp.asarray(a - 1, F32)
        step_b = jnp.asarray(b - 1, F32)
        moved = jnp.where(is_x, step_a, jnp.where(is_y, step_b, 0.0))

        def some_tiles(group, carry, piece=piece, base=(3 * a + b) * tiles, moved=moved):
            for u in range(unroll):
                at = group * unroll + u
                tile = piece[pl.ds(pl.multiple_of(at * 8, 8), 8), :]
                features, moments = source_tile(tile, moved, is_mass, low_half)
                for half in range(2):
                    feature[2 * (base + at) + half] = features[half]
                    moment[2 * (base + at) + half] = moments[half]
            return carry

        lax.fori_loop(0, tiles // unroll, some_tiles, 0)


def start_rows(*refs, places, count_blocks):
    pieces, (feature, moment, target, centre) = refs[:-4], refs[-4:]
    slots, width = centre.shape[1:]
    own = pieces[0]
    line = lax.broadcasted_iota(jnp.int32, (8, width), 0)
    is_mass, low_half = line % 4 == 3, line < 4

    def one_target(pair, carry):
        tile = own[pl.ds(pl.multiple_of(pair * 8, 8), 8), :]
        for half, value in enumerate(target_tile(tile, is_mass, low_half)):
            target[2 * pair + half] = value
        return carry

    lax.fori_loop(0, slots // 2, one_target, 0)
    for c in range(3):
        centre[c] = own[pl.ds(c, slots, stride=4), :] - middle
    add_sources(pieces, places, feature, moment, count_blocks)


def more_rows(feature_in, moment_in, *refs, places, count_blocks):
    pieces, (feature, moment) = refs[:-2], refs[-2:]
    add_sources(pieces, places, feature, moment, count_blocks)


def last_rows(feature_in, moment_in, *refs, places, count_blocks, here, there):
    pieces, (feature, moment, here_mass, there_mass) = refs[:-4], refs[-4:]
    width = feature.shape[2]
    for row in range(here_mass.shape[0] // width):
        for out, members in ((here_mass, here), (there_mass, there)):
            values = [pieces[k][count_blocks * 4 + row, :] for k in members]
            out[pl.ds(row * width, width)] = functools.reduce(jnp.add, values)
    add_sources(pieces[: len(places)], places, feature, moment, count_blocks)


def pair_sums(first, count, limit, lists, feature, moment, target, centre, out, together):
    entries = lists.shape[0]

    def some_slots(group, carry):
        for u in range(together):
            at = group * together + u
            slot = first + at
            near = target[slot]
            sums = jnp.zeros((moment.shape[1], moment.shape[2]), F32)
            for k in range(0, entries, 2):
                one, two = lists[k, slot], lists[k + 1, slot]
                here = jnp.concatenate([feature[one], feature[two]], axis=1)
                parts = jnp.concatenate([moment[one], moment[two]], axis=1)
                dist_sq = lax.dot_general(here, near, (((0,), (0,)), ((), ())), preferred_element_type=F32)
                inverse = lax.rsqrt(dist_sq)
                weight = inverse * inverse * inverse
                high = weight.astype(BF16)
                low = (weight - high.astype(F32)).astype(BF16)
                sums += jnp.dot(parts, high, preferred_element_type=F32)
                sums += jnp.dot(parts, low, preferred_element_type=F32)
            sums = (sums[0:4] + sums[4:8]) + sums[8:12]
            for c in range(3):
                own = centre[c, pl.ds(slot, 1), :]
                out[c, pl.ds(at, 1), :] = sums[c : c + 1] - own * sums[3:4]
        return carry

    groups = jnp.clip(limit - first + together - 1, 0, count) // together
    lax.fori_loop(0, groups, some_slots, 0)


def near_forces(lists_in, tie, limit, feature, moment, target, centre, out, lists, sem, *, first, together):
    copy = pltpu.make_async_copy(lists_in, lists, sem)
    copy.start()
    limit = jnp.max(limit[...].astype(F32)).astype(jnp.int32)
    copy.wait()
    pair_sums(first, out.shape[1], limit, lists, feature, moment, target, centre, out, together)


def add_far(some_mass, more_mass, limit, centre, *refs, half_gy, total, unroll):
    nears, out, masses, sems = refs[:-3], *refs[-3:]
    slots, width = out.shape[1:]
    copies = [
        pltpu.make_async_copy(some_mass, masses.at[0], sems.at[0]),
        pltpu.make_async_copy(more_mass, masses.at[1], sems.at[1]),
    ]
    for copy in copies:
        copy.start()
    for copy in copies:
        copy.wait()
    corner = (lax.axis_index("gx").astype(F32) + middle, lax.axis_index("gy").astype(F32) + middle, middle)
    position = [centre[c] + corner[c] for c in range(3)]

    def cells(step, carry):
        for u in range(unroll):
            cell = step * unroll + u
            group, sub_cell = cell // SUBC, cell % SUBC
            centre = (
                (2 * (group // half_gy) + 1).astype(F32),
                (2 * (group % half_gy) + 1).astype(F32),
                (sub_cell.astype(F32) + 0.5) * (1.0 / SUBC),
            )
            offset = [centre[c] - position[c] for c in range(3)]
            dist_sq = (offset[0] * offset[0] + offset[1] * offset[1]) + offset[2] * offset[2]
            inverse = lax.rsqrt(dist_sq + soft_far * soft_far)
            weight = (masses[0, cell] + masses[1, cell]) * (inverse * inverse * inverse)
            carry = tuple(carry[c] + weight * offset[c] for c in range(3))
        return carry

    far = lax.fori_loop(0, total // unroll, cells, tuple(jnp.zeros_like(v) for v in position))
    active = lax.broadcasted_iota(jnp.int32, (slots, width), 0) < limit[...]
    for c in range(3):
        near = jnp.concatenate([piece[c] for piece in nears], axis=0)
        out[c] = jnp.where(active, near + far[c], 0.0)


def body(blocks, active_counts, pair_lists, cell_ids):
    count_blocks, width = blocks.shape[2], blocks.shape[4]
    slots, entries = pair_lists.shape[2:]
    half_gy = lax.axis_size("gy") // 2
    total = lax.axis_size("gx") // 2 * half_gy * SUBC
    own = blocks.reshape(count_blocks * 4, width)
    smem = pl.BlockSpec(memory_space=pltpu.SMEM)
    vmem = pl.BlockSpec(memory_space=pltpu.VMEM)

    lines = -(-total // width)
    rows = count_blocks * 4
    hbm = pl.BlockSpec(memory_space=pl.ANY)
    marked = pl.pallas_call(
        functools.partial(mark, half_gy=half_gy),
        out_shape=jax.ShapeDtypeStruct((rows + 8 * -(-lines // 8), width), F32),
        in_specs=[hbm] * 2,
        out_specs=vmem,
        scratch_shapes=[pltpu.VMEM((1, count_blocks), jnp.int32), pltpu.SemaphoreType.DMA((2,))],
        compiler_params=pltpu.CompilerParams(vmem_limit_bytes=2 * 2**20),
    )(own, cell_ids[0])
    lists = pair_lists[0, 0].T

    first_x = swap(marked, "gx", 0)
    second_y = swap(marked, "gy", 1)
    first_y = swap(marked, "gy", 0)
    second_x = swap(lax.optimization_barrier((own, marked))[0], "gx", 1)
    row_params = dict(
        compiler_params=pltpu.CompilerParams(vmem_limit_bytes=16 * 2**20),
        cost_estimate=pl.CostEstimate(flops=1, bytes_accessed=1, transcendentals=0),
    )
    table = list(pl.pallas_call(
        functools.partial(start_rows, places=[(0, 0)], count_blocks=count_blocks),
        out_shape=[
            jax.ShapeDtypeStruct((9 * count_blocks, 32, width), BF16),
            jax.ShapeDtypeStruct((9 * count_blocks, 16, width), BF16),
            jax.ShapeDtypeStruct((slots, 32, width), BF16),
            jax.ShapeDtypeStruct((3, slots, width), F32),
        ],
        in_specs=[vmem],
        out_specs=[vmem] * 4,
        **row_params,
    )(marked))

    second_x = second_x
    first_x = lax.optimization_barrier((first_x, table[3]))[0]
    first_xy = swap(first_x, "gy", 0)
    first_xyy = swap(first_x, "gy", 1)

    table[:2] = pl.pallas_call(
        functools.partial(more_rows, places=[(1, 0), (0, 1), (0, 2)], count_blocks=count_blocks),
        out_shape=table[:2],
        in_specs=[vmem] * 5,
        out_specs=[vmem] * 2,
        input_output_aliases={0: 0, 1: 1},
        **row_params,
    )(*table[:2], first_x, first_y, second_y)

    second_xy = swap(second_x, "gy", 0)
    second_xyy = swap(second_x, "gy", 1)
    more = [first_xy, second_x, second_xy, first_xyy, marked, first_x, first_y, second_y]
    *rows_now, here_mass, there_mass = pl.pallas_call(
        functools.partial(
            last_rows,
            places=[(1, 1), (2, 0), (2, 1), (1, 2)],
            count_blocks=count_blocks,
            here=(0, 4, 5, 6),
            there=(3, 7),
        ),
        out_shape=[*table[:2]] + [jax.ShapeDtypeStruct((lines * width,), F32)] * 2,
        in_specs=[vmem] * (2 + len(more)),
        out_specs=[vmem] * 4,
        input_output_aliases={0: 0, 1: 1},
        **row_params,
    )(*table[:2], *more)
    table = [*rows_now, *table[2:]]
    table[:2] = pl.pallas_call(
        functools.partial(more_rows, places=[(2, 2)], count_blocks=count_blocks),
        out_shape=table[:2],
        in_specs=[vmem] * 3,
        out_specs=[vmem] * 2,
        input_output_aliases={0: 0, 1: 1},
        compiler_params=row_params["compiler_params"],
        cost_estimate=pl.CostEstimate(flops=5 * 10**9, bytes_accessed=1, transcendentals=0),
    )(*table[:2], second_xyy)

    together = math.gcd(slots, 8)
    ranges = split_slots(slots, together)

    def near_part(k, tie):
        first, count = ranges[k]
        return pl.pallas_call(
            functools.partial(near_forces, first=first, together=math.gcd(count, 24 if count % 24 == 0 else 8)),
            out_shape=jax.ShapeDtypeStruct((3, count, width), F32),
            in_specs=[hbm] * 2 + [vmem] * 5,
            out_specs=vmem,
            scratch_shapes=[pltpu.SMEM((entries, slots), jnp.int32), pltpu.SemaphoreType.DMA],
            compiler_params=pltpu.CompilerParams(vmem_limit_bytes=16 * 2**20),
            cost_estimate=near_cost(count, entries, width),
        )(lists, tie, active_counts, *table)

    if lax.axis_size("gy") == 4:
        values = (here_mass + there_mass) + exchange(there_mass, "gy", 1)
        steps = []
    else:
        values = here_mass
        steps = [("gy", 2 << k) for k in range((lax.axis_size("gy") // 2).bit_length() - 1)]
    steps += [("gx", 2 << k) for k in range((lax.axis_size("gx") // 2).bit_length() - 1)]
    nears, parts = [], (values, jnp.zeros_like(values))
    for k, (axis, step) in enumerate(steps):
        values = lax.optimization_barrier((values, nears[-1] if nears else table[0]))[0]
        other = exchange(values, axis, step)
        parts = (values, other)
        if k >= len(steps) - 2 and len(nears) < len(ranges):
            nears.append(near_part(len(nears), values))
        values = values + other
    while len(nears) < len(ranges):
        nears.append(near_part(len(nears), parts[0]))

    result = pl.pallas_call(
        functools.partial(add_far, half_gy=half_gy, total=total, unroll=math.gcd(total, 16)),
        out_shape=jax.ShapeDtypeStruct((3, slots, width), F32),
        in_specs=[hbm] * 2 + [vmem] * (2 + len(nears)),
        out_specs=vmem,
        scratch_shapes=[
            pltpu.SMEM((2, lines * width), F32),
            pltpu.SemaphoreType.DMA((2,)),
        ],
        compiler_params=pltpu.CompilerParams(vmem_limit_bytes=4 * 2**20),
    )(*parts, active_counts, table[3], *nears)
    return result.transpose(1, 0, 2)[None, None]


def solution(mesh):
    in_specs = (
        P("gx", "gy", None, None, None),
        P("gx", "gy"),
        P("gx", "gy", None, None),
        P("gx", "gy", None),
    )
    out_specs = P("gx", "gy", None, None, None)
    return jax.shard_map(body, mesh=mesh, in_specs=in_specs, out_specs=out_specs, check_vma=False)
```

```python
import functools
import math

import jax
import jax.numpy as jnp
from jax import lax
from jax.experimental import pallas as pl
from jax.experimental.pallas import tpu as pltpu
from jax.sharding import PartitionSpec as P

SUBC = 2
F32 = jnp.float32
BF16 = jnp.bfloat16

soft_near = 0.05
soft_far = 1.0
middle = 0.5


def swap(block, axis, odd):
    count = lax.axis_size(axis)
    pairs = []
    for low in range(odd, count, 2):
        high = (low + 1) % count
        pairs += [(low, high), (high, low)]
    return lax.ppermute(block, axis, pairs)


def exchange(values, axis, step):
    return lax.ppermute(values, axis, [(i, i ^ step) for i in range(lax.axis_size(axis))])


def split_slots(slots, together):
    groups = slots // together
    cuts = [0, max(1, groups // 4), groups]
    return [(a * together, (b - a) * together) for a, b in zip(cuts, cuts[1:]) if b > a]


def near_cost(slots, entries, width):
    pairs = slots * entries * width * width
    return pl.CostEstimate(flops=20 * pairs, bytes_accessed=3 * slots * width * 4, transcendentals=pairs)


def split3(v):
    high = v.astype(BF16).astype(F32)
    rest = v - high
    mid = rest.astype(BF16).astype(F32)
    return high, mid, rest - mid


def roll(v, step):
    return pltpu.roll(v, step, 0)


def halves(low_half, pairs):
    upper, lower = [], []
    for (first, first_rolled), second in pairs:
        second, second_rolled = second or (jnp.zeros_like(first),) * 2
        upper.append(jnp.where(low_half, first, second_rolled))
        lower.append(jnp.where(low_half, first_rolled, second))
    return upper, lower


def rows16(tiles):
    return jnp.concatenate(tiles, axis=0).astype(BF16)


def with_rolled(v):
    return v, roll(v, 4)


def masked(is_mass, value, pair):
    return tuple(jnp.where(is_mass, value, v) for v in pair)


def square_norm(is_mass, centred):
    square = jnp.where(is_mass, 0.0, centred)
    square = square * square
    square = square + roll(square, 1)
    return square + roll(square, 2)


def source_tile(tile, moved, is_mass, low_half):
    centred = (tile + moved) - jnp.where(is_mass, 0.0, middle)
    rows = jnp.where(is_mass, square_norm(is_mass, centred), -2.0 * centred)
    high, mid, low = map(with_rolled, split3(rows))
    high_1, mid_1 = masked(is_mass, 1.0, high), masked(is_mass, 1.0, mid)
    features = halves(low_half, [(high, high_1), (high_1, mid), (mid_1, low)])
    zero = jnp.zeros_like(tile)
    mass = jnp.where(is_mass, tile, 0.0)
    mass = mass + roll(mass, 7)
    mass = mass + roll(mass, 6)
    high, mid, low = map(with_rolled, split3(jnp.where(is_mass, 1.0, centred) * mass))
    moments = halves(low_half, [(high, mid), (low, None)])
    return [rows16([*v, zero]) for v in features], [rows16(v) for v in moments]


def target_tile(tile, is_mass, low_half):
    centred = tile - middle
    norm = square_norm(is_mass, centred) + soft_near * soft_near
    high, mid, low = map(with_rolled, split3(jnp.where(is_mass, norm, centred)))
    one_high = masked(is_mass, 1.0, high)
    high_mid = tuple(jnp.where(is_mass, a, b) for a, b in zip(high, mid))
    mid_low = tuple(jnp.where(is_mass, a, b) for a, b in zip(mid, low))
    low_mid = tuple(jnp.where(is_mass, a, b) for a, b in zip(low, mid))
    groups = halves(low_half, [(one_high, high_mid), (mid_low, one_high), (low_mid, one_high)])
    return [rows16([*v, jnp.zeros_like(tile)]) for v in groups]


def mark(blocks, ids_in, out, ids, sems, *, half_gy):
    rows, width = blocks.shape
    copies = [
        pltpu.make_async_copy(ids_in, ids, sems.at[0]),
        pltpu.make_async_copy(blocks, out.at[pl.ds(0, rows), :], sems.at[1]),
    ]
    for copy in copies:
        copy.start()
    for copy in copies:
        copy.wait()
    first = (lax.axis_index("gx") // 2 * half_gy + lax.axis_index("gy") // 2) * SUBC
    count = ids.shape[1]
    line = lax.broadcasted_iota(jnp.int32, (8, count), 0)
    member = jnp.where(ids[...] - first == line, 1.0, 0.0)
    mass = out[pl.ds(3, count, stride=4), :]
    sums = jnp.dot(member, mass, preferred_element_type=F32, precision=lax.Precision.HIGHEST)
    sums = jnp.sum(sums, axis=1, keepdims=True)
    shape = (out.shape[0] - rows, width)
    cell = lax.broadcasted_iota(jnp.int32, shape, 0) * width + lax.broadcasted_iota(jnp.int32, shape, 1)
    values = jnp.zeros(shape, F32)
    for h in range(SUBC):
        values = jnp.where(cell == first + h, jnp.broadcast_to(sums[h : h + 1], shape), values)
    out[rows:, :] = values


def add_sources(pieces, places, feature, moment, count_blocks):
    width = feature.shape[2]
    even_x, even_y = 1 - lax.axis_index("gx") % 2, 1 - lax.axis_index("gy") % 2
    line = lax.broadcasted_iota(jnp.int32, (8, width), 0)
    is_mass, low_half = line % 4 == 3, line < 4
    is_x, is_y = line % 4 == 0, line % 4 == 1
    tiles = count_blocks // 2
    unroll = math.gcd(tiles, 8)
    for piece, (row, col) in zip(pieces, places):
        a = (1, 2 * even_x, 2 - 2 * even_x)[row]
        b = (1, 2 * even_y, 2 - 2 * even_y)[col]
        step_a = jnp.asarray(a - 1, F32)
        step_b = jnp.asarray(b - 1, F32)
        moved = jnp.where(is_x, step_a, jnp.where(is_y, step_b, 0.0))

        def some_tiles(group, carry, piece=piece, base=(3 * a + b) * tiles, moved=moved):
            for u in range(unroll):
                at = group * unroll + u
                tile = piece[pl.ds(pl.multiple_of(at * 8, 8), 8), :]
                features, moments = source_tile(tile, moved, is_mass, low_half)
                for half in range(2):
                    feature[2 * (base + at) + half] = features[half]
                    moment[2 * (base + at) + half] = moments[half]
            return carry

        lax.fori_loop(0, tiles // unroll, some_tiles, 0)


def start_rows(*refs, places, count_blocks):
    pieces, (feature, moment, target, centre) = refs[:-4], refs[-4:]
    slots, width = centre.shape[1:]
    own = pieces[0]
    line = lax.broadcasted_iota(jnp.int32, (8, width), 0)
    is_mass, low_half = line % 4 == 3, line < 4

    def one_target(pair, carry):
        tile = own[pl.ds(pl.multiple_of(pair * 8, 8), 8), :]
        for half, value in enumerate(target_tile(tile, is_mass, low_half)):
            target[2 * pair + half] = value
        return carry

    lax.fori_loop(0, slots // 2, one_target, 0)
    for c in range(3):
        centre[c] = own[pl.ds(c, slots, stride=4), :] - middle
    add_sources(pieces, places, feature, moment, count_blocks)


def more_rows(feature_in, moment_in, *refs, places, count_blocks):
    pieces, (feature, moment) = refs[:-2], refs[-2:]
    add_sources(pieces, places, feature, moment, count_blocks)


def last_rows(feature_in, moment_in, *refs, places, count_blocks, here, there):
    pieces, (feature, moment, here_mass, there_mass) = refs[:-4], refs[-4:]
    width = feature.shape[2]
    for row in range(here_mass.shape[0] // width):
        for out, members in ((here_mass, here), (there_mass, there)):
            values = [pieces[k][count_blocks * 4 + row, :] for k in members]
            out[pl.ds(row * width, width)] = functools.reduce(jnp.add, values)
    add_sources(pieces[: len(places)], places, feature, moment, count_blocks)


def pair_sums(first, count, limit, lists, feature, moment, target, centre, out, together):
    entries = lists.shape[0]

    def some_slots(group, carry):
        for u in range(together):
            at = group * together + u
            slot = first + at
            near = target[slot]
            sums = jnp.zeros((moment.shape[1], moment.shape[2]), F32)
            for k in range(0, entries, 2):
                one, two = lists[k, slot], lists[k + 1, slot]
                here = jnp.concatenate([feature[one], feature[two]], axis=1)
                parts = jnp.concatenate([moment[one], moment[two]], axis=1)
                dist_sq = lax.dot_general(here, near, (((0,), (0,)), ((), ())), preferred_element_type=F32)
                inverse = lax.rsqrt(dist_sq)
                weight = inverse * inverse * inverse
                high = weight.astype(BF16)
                low = (weight - high.astype(F32)).astype(BF16)
                sums += jnp.dot(parts, high, preferred_element_type=F32)
                sums += jnp.dot(parts, low, preferred_element_type=F32)
            sums = (sums[0:4] + sums[4:8]) + sums[8:12]
            for c in range(3):
                own = centre[c, pl.ds(slot, 1), :]
                out[c, pl.ds(at, 1), :] = sums[c : c + 1] - own * sums[3:4]
        return carry

    groups = jnp.clip(limit - first + together - 1, 0, count) // together
    lax.fori_loop(0, groups, some_slots, 0)


def near_forces(lists_in, tie, limit, feature, moment, target, centre, out, lists, sem, *, first, together):
    copy = pltpu.make_async_copy(lists_in, lists, sem)
    copy.start()
    limit = jnp.max(limit[...].astype(F32)).astype(jnp.int32)
    copy.wait()
    pair_sums(first, out.shape[1], limit, lists, feature, moment, target, centre, out, together)


def add_far(some_mass, more_mass, limit, centre, *refs, half_gy, total):
    nears, out = refs[:-1], refs[-1]
    slots, width = out.shape[1:]
    corner = (lax.axis_index("gx").astype(F32) + middle, lax.axis_index("gy").astype(F32) + middle, middle)
    position = [centre[c] + corner[c] for c in range(3)]
    far = [jnp.zeros((slots, width), F32)] * 3
    for line in range(-(-total // width)):
        at = pl.ds(line * width, width)
        masses = (some_mass[at] + more_mass[at]).reshape(1, width)
        for cell in range(line * width, min(total, (line + 1) * width)):
            group, sub_cell = divmod(cell, SUBC)
            middle_of = (2.0 * (group // half_gy) + 1, 2.0 * (group % half_gy) + 1, (sub_cell + 0.5) / SUBC)
            offset = [middle_of[c] - position[c] for c in range(3)]
            dist_sq = (offset[0] * offset[0] + offset[1] * offset[1]) + offset[2] * offset[2]
            inverse = lax.rsqrt(dist_sq + soft_far * soft_far)
            lane = cell - line * width
            weight = masses[:, lane : lane + 1] * (inverse * inverse * inverse)
            far = [far[c] + weight * offset[c] for c in range(3)]
    active = lax.broadcasted_iota(jnp.int32, (slots, width), 0) < limit[...]
    for c in range(3):
        near = jnp.concatenate([piece[c] for piece in nears], axis=0)
        out[c] = jnp.where(active, near + far[c], 0.0)


def body(blocks, active_counts, pair_lists, cell_ids):
    count_blocks, width = blocks.shape[2], blocks.shape[4]
    slots, entries = pair_lists.shape[2:]
    half_gy = lax.axis_size("gy") // 2
    total = lax.axis_size("gx") // 2 * half_gy * SUBC
    own = blocks.reshape(count_blocks * 4, width)
    smem = pl.BlockSpec(memory_space=pltpu.SMEM)
    vmem = pl.BlockSpec(memory_space=pltpu.VMEM)

    lines = -(-total // width)
    rows = count_blocks * 4
    hbm = pl.BlockSpec(memory_space=pl.ANY)
    marked = pl.pallas_call(
        functools.partial(mark, half_gy=half_gy),
        out_shape=jax.ShapeDtypeStruct((rows + 8 * -(-lines // 8), width), F32),
        in_specs=[hbm] * 2,
        out_specs=vmem,
        scratch_shapes=[pltpu.VMEM((1, count_blocks), jnp.int32), pltpu.SemaphoreType.DMA((2,))],
        compiler_params=pltpu.CompilerParams(vmem_limit_bytes=2 * 2**20),
    )(own, cell_ids[0])
    lists = pair_lists[0, 0].T

    first_x = swap(marked, "gx", 0)
    second_y = swap(marked, "gy", 1)
    first_y = swap(marked, "gy", 0)
    second_x = swap(lax.optimization_barrier((own, marked))[0], "gx", 1)
    row_params = dict(
        compiler_params=pltpu.CompilerParams(vmem_limit_bytes=16 * 2**20),
        cost_estimate=pl.CostEstimate(flops=1, bytes_accessed=1, transcendentals=0),
    )
    table = list(pl.pallas_call(
        functools.partial(start_rows, places=[(0, 0)], count_blocks=count_blocks),
        out_shape=[
            jax.ShapeDtypeStruct((9 * count_blocks, 32, width), BF16),
            jax.ShapeDtypeStruct((9 * count_blocks, 16, width), BF16),
            jax.ShapeDtypeStruct((slots, 32, width), BF16),
            jax.ShapeDtypeStruct((3, slots, width), F32),
        ],
        in_specs=[vmem],
        out_specs=[vmem] * 4,
        **row_params,
    )(marked))

    second_x = second_x
    first_x = lax.optimization_barrier((first_x, table[3]))[0]
    first_xy = swap(first_x, "gy", 0)
    first_xyy = swap(first_x, "gy", 1)

    table[:2] = pl.pallas_call(
        functools.partial(more_rows, places=[(1, 0), (0, 1), (0, 2)], count_blocks=count_blocks),
        out_shape=table[:2],
        in_specs=[vmem] * 5,
        out_specs=[vmem] * 2,
        input_output_aliases={0: 0, 1: 1},
        **row_params,
    )(*table[:2], first_x, first_y, second_y)

    second_xy = swap(second_x, "gy", 0)
    second_xyy = swap(second_x, "gy", 1)
    more = [first_xy, second_x, second_xy, first_xyy, marked, first_x, first_y, second_y]
    *rows_now, here_mass, there_mass = pl.pallas_call(
        functools.partial(
            last_rows,
            places=[(1, 1), (2, 0), (2, 1), (1, 2)],
            count_blocks=count_blocks,
            here=(0, 4, 5, 6),
            there=(3, 7),
        ),
        out_shape=[*table[:2]] + [jax.ShapeDtypeStruct((lines * width,), F32)] * 2,
        in_specs=[vmem] * (2 + len(more)),
        out_specs=[vmem] * 4,
        input_output_aliases={0: 0, 1: 1},
        **row_params,
    )(*table[:2], *more)
    table = [*rows_now, *table[2:]]
    table[:2] = pl.pallas_call(
        functools.partial(more_rows, places=[(2, 2)], count_blocks=count_blocks),
        out_shape=table[:2],
        in_specs=[vmem] * 3,
        out_specs=[vmem] * 2,
        input_output_aliases={0: 0, 1: 1},
        compiler_params=row_params["compiler_params"],
        cost_estimate=pl.CostEstimate(flops=5 * 10**9, bytes_accessed=1, transcendentals=0),
    )(*table[:2], second_xyy)

    together = math.gcd(slots, 8)
    ranges = split_slots(slots, together)

    def near_part(k, tie):
        first, count = ranges[k]
        return pl.pallas_call(
            functools.partial(near_forces, first=first, together=math.gcd(count, 24 if count % 24 == 0 else 8)),
            out_shape=jax.ShapeDtypeStruct((3, count, width), F32),
            in_specs=[hbm] * 2 + [vmem] * 5,
            out_specs=vmem,
            scratch_shapes=[pltpu.SMEM((entries, slots), jnp.int32), pltpu.SemaphoreType.DMA],
            compiler_params=pltpu.CompilerParams(vmem_limit_bytes=16 * 2**20),
            cost_estimate=near_cost(count, entries, width),
        )(lists, tie, active_counts, *table)

    if lax.axis_size("gy") == 4:
        values = (here_mass + there_mass) + exchange(there_mass, "gy", 1)
        steps = []
    else:
        values = here_mass
        steps = [("gy", 2 << k) for k in range((lax.axis_size("gy") // 2).bit_length() - 1)]
    steps += [("gx", 2 << k) for k in range((lax.axis_size("gx") // 2).bit_length() - 1)]
    nears, parts = [], (values, jnp.zeros_like(values))
    for k, (axis, step) in enumerate(steps):
        values = lax.optimization_barrier((values, nears[-1] if nears else table[0]))[0]
        other = exchange(values, axis, step)
        parts = (values, other)
        if k >= len(steps) - 2 and len(nears) < len(ranges):
            nears.append(near_part(len(nears), values))
        values = values + other
    while len(nears) < len(ranges):
        nears.append(near_part(len(nears), parts[0]))

    result = pl.pallas_call(
        functools.partial(add_far, half_gy=half_gy, total=total),
        out_shape=jax.ShapeDtypeStruct((3, slots, width), F32),
        in_specs=[vmem] * (4 + len(nears)),
        out_specs=vmem,
        compiler_params=pltpu.CompilerParams(vmem_limit_bytes=12 * 2**20),
    )(*parts, active_counts, table[3], *nears)
    return result.transpose(1, 0, 2)[None, None]


def solution(mesh):
    in_specs = (
        P("gx", "gy", None, None, None),
        P("gx", "gy"),
        P("gx", "gy", None, None),
        P("gx", "gy", None),
    )
    out_specs = P("gx", "gy", None, None, None)
    return jax.shard_map(body, mesh=mesh, in_specs=in_specs, out_specs=out_specs, check_vma=False)
```

```python
import functools
import math

import jax
import jax.numpy as jnp
from jax import lax
from jax.experimental import pallas as pl
from jax.experimental.pallas import tpu as pltpu
from jax.sharding import PartitionSpec as P

SUBC = 2
F32 = jnp.float32
BF16 = jnp.bfloat16

soft_near = 0.05
soft_far = 1.0
middle = 0.5


def swap(block, axis, odd):
    count = lax.axis_size(axis)
    pairs = []
    for low in range(odd, count, 2):
        high = (low + 1) % count
        pairs += [(low, high), (high, low)]
    return lax.ppermute(block, axis, pairs)


def exchange(values, axis, step):
    return lax.ppermute(values, axis, [(i, i ^ step) for i in range(lax.axis_size(axis))])


def split_slots(slots, together):
    groups = slots // together
    cuts = [0, max(1, groups // 2), groups]
    return [(a * together, (b - a) * together) for a, b in zip(cuts, cuts[1:]) if b > a]


def near_cost(slots, entries, width):
    pairs = slots * entries * width * width
    return pl.CostEstimate(flops=20 * pairs, bytes_accessed=3 * slots * width * 4, transcendentals=pairs)


def split3(v):
    high = v.astype(BF16).astype(F32)
    rest = v - high
    mid = rest.astype(BF16).astype(F32)
    return high, mid, rest - mid


def roll(v, step):
    return pltpu.roll(v, step, 0)


def halves(low_half, pairs):
    upper, lower = [], []
    for (first, first_rolled), second in pairs:
        second, second_rolled = second or (jnp.zeros_like(first),) * 2
        upper.append(jnp.where(low_half, first, second_rolled))
        lower.append(jnp.where(low_half, first_rolled, second))
    return upper, lower


def rows16(tiles):
    return jnp.concatenate(tiles, axis=0).astype(BF16)


def with_rolled(v):
    return v, roll(v, 4)


def masked(is_mass, value, pair):
    return tuple(jnp.where(is_mass, value, v) for v in pair)


def square_norm(is_mass, centred):
    square = jnp.where(is_mass, 0.0, centred)
    square = square * square
    square = square + roll(square, 1)
    return square + roll(square, 2)


def source_tile(tile, moved, is_mass, low_half):
    centred = (tile + moved) - jnp.where(is_mass, 0.0, middle)
    rows = jnp.where(is_mass, square_norm(is_mass, centred), -2.0 * centred)
    high, mid, low = map(with_rolled, split3(rows))
    high_1, mid_1 = masked(is_mass, 1.0, high), masked(is_mass, 1.0, mid)
    features = halves(low_half, [(high, high_1), (high_1, mid), (mid_1, low)])
    zero = jnp.zeros_like(tile)
    mass = jnp.where(is_mass, tile, 0.0)
    mass = mass + roll(mass, 7)
    mass = mass + roll(mass, 6)
    high, mid, low = map(with_rolled, split3(jnp.where(is_mass, 1.0, centred) * mass))
    moments = halves(low_half, [(high, mid), (low, None)])
    return [rows16([*v, zero]) for v in features], [rows16(v) for v in moments]


def target_tile(tile, is_mass, low_half):
    centred = tile - middle
    norm = square_norm(is_mass, centred) + soft_near * soft_near
    high, mid, low = map(with_rolled, split3(jnp.where(is_mass, norm, centred)))
    one_high = masked(is_mass, 1.0, high)
    high_mid = tuple(jnp.where(is_mass, a, b) for a, b in zip(high, mid))
    mid_low = tuple(jnp.where(is_mass, a, b) for a, b in zip(mid, low))
    low_mid = tuple(jnp.where(is_mass, a, b) for a, b in zip(low, mid))
    groups = halves(low_half, [(one_high, high_mid), (mid_low, one_high), (low_mid, one_high)])
    return [rows16([*v, jnp.zeros_like(tile)]) for v in groups]


def mark(blocks, ids_in, out, ids, sems, *, half_gy):
    rows, width = blocks.shape
    copies = [
        pltpu.make_async_copy(ids_in, ids, sems.at[0]),
        pltpu.make_async_copy(blocks, out.at[pl.ds(0, rows), :], sems.at[1]),
    ]
    for copy in copies:
        copy.start()
    for copy in copies:
        copy.wait()
    first = (lax.axis_index("gx") // 2 * half_gy + lax.axis_index("gy") // 2) * SUBC
    count = ids.shape[1]
    line = lax.broadcasted_iota(jnp.int32, (8, count), 0)
    member = jnp.where(ids[...] - first == line, 1.0, 0.0)
    mass = out[pl.ds(3, count, stride=4), :]
    sums = jnp.dot(member, mass, preferred_element_type=F32, precision=lax.Precision.HIGHEST)
    sums = jnp.sum(sums, axis=1, keepdims=True)
    shape = (out.shape[0] - rows, width)
    cell = lax.broadcasted_iota(jnp.int32, shape, 0) * width + lax.broadcasted_iota(jnp.int32, shape, 1)
    values = jnp.zeros(shape, F32)
    for h in range(SUBC):
        values = jnp.where(cell == first + h, jnp.broadcast_to(sums[h : h + 1], shape), values)
    out[rows:, :] = values


def add_sources(pieces, places, feature, moment, count_blocks):
    width = feature.shape[2]
    even_x, even_y = 1 - lax.axis_index("gx") % 2, 1 - lax.axis_index("gy") % 2
    line = lax.broadcasted_iota(jnp.int32, (8, width), 0)
    is_mass, low_half = line % 4 == 3, line < 4
    is_x, is_y = line % 4 == 0, line % 4 == 1
    tiles = count_blocks // 2
    unroll = math.gcd(tiles, 8)
    for piece, (row, col) in zip(pieces, places):
        a = (1, 2 * even_x, 2 - 2 * even_x)[row]
        b = (1, 2 * even_y, 2 - 2 * even_y)[col]
        step_a = jnp.asarray(a - 1, F32)
        step_b = jnp.asarray(b - 1, F32)
        moved = jnp.where(is_x, step_a, jnp.where(is_y, step_b, 0.0))

        def some_tiles(group, carry, piece=piece, base=(3 * a + b) * tiles, moved=moved):
            for u in range(unroll):
                at = group * unroll + u
                tile = piece[pl.ds(pl.multiple_of(at * 8, 8), 8), :]
                features, moments = source_tile(tile, moved, is_mass, low_half)
                for half in range(2):
                    feature[2 * (base + at) + half] = features[half]
                    moment[2 * (base + at) + half] = moments[half]
            return carry

        lax.fori_loop(0, tiles // unroll, some_tiles, 0)


def start_rows(*refs, places, count_blocks):
    pieces, (feature, moment, target, centre) = refs[:-4], refs[-4:]
    slots, width = centre.shape[1:]
    own = pieces[0]
    line = lax.broadcasted_iota(jnp.int32, (8, width), 0)
    is_mass, low_half = line % 4 == 3, line < 4

    def one_target(pair, carry):
        tile = own[pl.ds(pl.multiple_of(pair * 8, 8), 8), :]
        for half, value in enumerate(target_tile(tile, is_mass, low_half)):
            target[2 * pair + half] = value
        return carry

    lax.fori_loop(0, slots // 2, one_target, 0)
    for c in range(3):
        centre[c] = own[pl.ds(c, slots, stride=4), :] - middle
    add_sources(pieces, places, feature, moment, count_blocks)


def more_rows(feature_in, moment_in, *refs, places, count_blocks):
    pieces, (feature, moment) = refs[:-2], refs[-2:]
    add_sources(pieces, places, feature, moment, count_blocks)


def last_rows(feature_in, moment_in, *refs, places, count_blocks, here, there):
    pieces, (feature, moment, here_mass, there_mass) = refs[:-4], refs[-4:]
    width = feature.shape[2]
    for row in range(here_mass.shape[0] // width):
        for out, members in ((here_mass, here), (there_mass, there)):
            values = [pieces[k][count_blocks * 4 + row, :] for k in members]
            out[pl.ds(row * width, width)] = functools.reduce(jnp.add, values)
    add_sources(pieces[: len(places)], places, feature, moment, count_blocks)


def pair_sums(first, count, limit, lists, feature, moment, target, centre, out, together):
    entries = lists.shape[0]

    def some_slots(group, carry):
        for u in range(together):
            at = group * together + u
            slot = first + at
            near = target[slot]
            sums = jnp.zeros((moment.shape[1], moment.shape[2]), F32)
            for k in range(0, entries, 2):
                one, two = lists[k, slot], lists[k + 1, slot]
                here = jnp.concatenate([feature[one], feature[two]], axis=1)
                parts = jnp.concatenate([moment[one], moment[two]], axis=1)
                dist_sq = lax.dot_general(here, near, (((0,), (0,)), ((), ())), preferred_element_type=F32)
                inverse = lax.rsqrt(dist_sq)
                weight = inverse * inverse * inverse
                high = weight.astype(BF16)
                low = (weight - high.astype(F32)).astype(BF16)
                sums += jnp.dot(parts, high, preferred_element_type=F32)
                sums += jnp.dot(parts, low, preferred_element_type=F32)
            sums = (sums[0:4] + sums[4:8]) + sums[8:12]
            for c in range(3):
                own = centre[c, pl.ds(slot, 1), :]
                out[c, pl.ds(at, 1), :] = sums[c : c + 1] - own * sums[3:4]
        return carry

    groups = jnp.clip(limit - first + together - 1, 0, count) // together
    lax.fori_loop(0, groups, some_slots, 0)


def near_forces(lists_in, tie, limit, feature, moment, target, centre, out, lists, sem, *, first, together):
    copy = pltpu.make_async_copy(lists_in, lists, sem)
    copy.start()
    limit = jnp.max(limit[...].astype(F32)).astype(jnp.int32)
    copy.wait()
    pair_sums(first, out.shape[1], limit, lists, feature, moment, target, centre, out, together)


def add_far(some_mass, more_mass, limit, centre, *refs, half_gy, total):
    nears, out = refs[:-1], refs[-1]
    slots, width = out.shape[1:]
    corner = (lax.axis_index("gx").astype(F32) + middle, lax.axis_index("gy").astype(F32) + middle, middle)
    position = [centre[c] + corner[c] for c in range(3)]
    far = [jnp.zeros((slots, width), F32)] * 3
    for line in range(-(-total // width)):
        at = pl.ds(line * width, width)
        masses = (some_mass[at] + more_mass[at]).reshape(1, width)
        for cell in range(line * width, min(total, (line + 1) * width)):
            group, sub_cell = divmod(cell, SUBC)
            middle_of = (2.0 * (group // half_gy) + 1, 2.0 * (group % half_gy) + 1, (sub_cell + 0.5) / SUBC)
            offset = [middle_of[c] - position[c] for c in range(3)]
            dist_sq = (offset[0] * offset[0] + offset[1] * offset[1]) + offset[2] * offset[2]
            inverse = lax.rsqrt(dist_sq + soft_far * soft_far)
            lane = cell - line * width
            weight = masses[:, lane : lane + 1] * (inverse * inverse * inverse)
            far = [far[c] + weight * offset[c] for c in range(3)]
    active = lax.broadcasted_iota(jnp.int32, (slots, width), 0) < limit[...]
    for c in range(3):
        near = jnp.concatenate([piece[c] for piece in nears], axis=0)
        out[c] = jnp.where(active, near + far[c], 0.0)


def body(blocks, active_counts, pair_lists, cell_ids):
    count_blocks, width = blocks.shape[2], blocks.shape[4]
    slots, entries = pair_lists.shape[2:]
    half_gy = lax.axis_size("gy") // 2
    total = lax.axis_size("gx") // 2 * half_gy * SUBC
    own = blocks.reshape(count_blocks * 4, width)
    smem = pl.BlockSpec(memory_space=pltpu.SMEM)
    vmem = pl.BlockSpec(memory_space=pltpu.VMEM)

    lines = -(-total // width)
    rows = count_blocks * 4
    hbm = pl.BlockSpec(memory_space=pl.ANY)
    marked = pl.pallas_call(
        functools.partial(mark, half_gy=half_gy),
        out_shape=jax.ShapeDtypeStruct((rows + 8 * -(-lines // 8), width), F32),
        in_specs=[hbm] * 2,
        out_specs=vmem,
        scratch_shapes=[pltpu.VMEM((1, count_blocks), jnp.int32), pltpu.SemaphoreType.DMA((2,))],
        compiler_params=pltpu.CompilerParams(vmem_limit_bytes=2 * 2**20),
    )(own, cell_ids[0])
    lists = pair_lists[0, 0].T

    first_x = swap(marked, "gx", 0)
    second_y = swap(marked, "gy", 1)
    first_y = swap(marked, "gy", 0)
    second_x = swap(lax.optimization_barrier((own, marked))[0], "gx", 1)
    row_params = dict(
        compiler_params=pltpu.CompilerParams(vmem_limit_bytes=16 * 2**20),
        cost_estimate=pl.CostEstimate(flops=1, bytes_accessed=1, transcendentals=0),
    )
    table = list(pl.pallas_call(
        functools.partial(start_rows, places=[(0, 0)], count_blocks=count_blocks),
        out_shape=[
            jax.ShapeDtypeStruct((9 * count_blocks, 32, width), BF16),
            jax.ShapeDtypeStruct((9 * count_blocks, 16, width), BF16),
            jax.ShapeDtypeStruct((slots, 32, width), BF16),
            jax.ShapeDtypeStruct((3, slots, width), F32),
        ],
        in_specs=[vmem],
        out_specs=[vmem] * 4,
        **row_params,
    )(marked))

    second_x = second_x
    first_x = lax.optimization_barrier((first_x, table[3]))[0]
    first_xy = swap(first_x, "gy", 0)
    first_xyy = swap(first_x, "gy", 1)

    table[:2] = pl.pallas_call(
        functools.partial(more_rows, places=[(1, 0), (0, 1), (0, 2)], count_blocks=count_blocks),
        out_shape=table[:2],
        in_specs=[vmem] * 5,
        out_specs=[vmem] * 2,
        input_output_aliases={0: 0, 1: 1},
        **row_params,
    )(*table[:2], first_x, first_y, second_y)

    second_xy = swap(second_x, "gy", 0)
    second_xyy = swap(second_x, "gy", 1)
    more = [first_xy, second_x, second_xy, first_xyy, marked, first_x, first_y, second_y]
    *rows_now, here_mass, there_mass = pl.pallas_call(
        functools.partial(
            last_rows,
            places=[(1, 1), (2, 0), (2, 1), (1, 2)],
            count_blocks=count_blocks,
            here=(0, 4, 5, 6),
            there=(3, 7),
        ),
        out_shape=[*table[:2]] + [jax.ShapeDtypeStruct((lines * width,), F32)] * 2,
        in_specs=[vmem] * (2 + len(more)),
        out_specs=[vmem] * 4,
        input_output_aliases={0: 0, 1: 1},
        **row_params,
    )(*table[:2], *more)
    table = [*rows_now, *table[2:]]
    table[:2] = pl.pallas_call(
        functools.partial(more_rows, places=[(2, 2)], count_blocks=count_blocks),
        out_shape=table[:2],
        in_specs=[vmem] * 3,
        out_specs=[vmem] * 2,
        input_output_aliases={0: 0, 1: 1},
        compiler_params=row_params["compiler_params"],
        cost_estimate=pl.CostEstimate(flops=5 * 10**9, bytes_accessed=1, transcendentals=0),
    )(*table[:2], second_xyy)

    together = math.gcd(slots, 8)
    ranges = split_slots(slots, together)

    def near_part(k, tie):
        first, count = ranges[k]
        return pl.pallas_call(
            functools.partial(near_forces, first=first, together=math.gcd(count, 16)),
            out_shape=jax.ShapeDtypeStruct((3, count, width), F32),
            in_specs=[hbm] * 2 + [vmem] * 5,
            out_specs=vmem,
            scratch_shapes=[pltpu.SMEM((entries, slots), jnp.int32), pltpu.SemaphoreType.DMA],
            compiler_params=pltpu.CompilerParams(vmem_limit_bytes=16 * 2**20),
            cost_estimate=near_cost(count, entries, width),
        )(lists, tie, active_counts, *table)

    if lax.axis_size("gy") == 4:
        values = (here_mass + there_mass) + exchange(there_mass, "gy", 1)
        steps = []
    else:
        values = here_mass
        steps = [("gy", 2 << k) for k in range((lax.axis_size("gy") // 2).bit_length() - 1)]
    steps += [("gx", 2 << k) for k in range((lax.axis_size("gx") // 2).bit_length() - 1)]
    nears, parts = [], (values, jnp.zeros_like(values))
    for k, (axis, step) in enumerate(steps):
        values = lax.optimization_barrier((values, nears[-1] if nears else table[0]))[0]
        other = exchange(values, axis, step)
        parts = (values, other)
        if k >= len(steps) - 2 and len(nears) < len(ranges):
            nears.append(near_part(len(nears), values))
        values = values + other
    while len(nears) < len(ranges):
        nears.append(near_part(len(nears), parts[0]))

    result = pl.pallas_call(
        functools.partial(add_far, half_gy=half_gy, total=total),
        out_shape=jax.ShapeDtypeStruct((3, slots, width), F32),
        in_specs=[vmem] * (4 + len(nears)),
        out_specs=vmem,
        compiler_params=pltpu.CompilerParams(vmem_limit_bytes=12 * 2**20),
    )(*parts, active_counts, table[3], *nears)
    return result.transpose(1, 0, 2)[None, None]


def solution(mesh):
    in_specs = (
        P("gx", "gy", None, None, None),
        P("gx", "gy"),
        P("gx", "gy", None, None),
        P("gx", "gy", None),
    )
    out_specs = P("gx", "gy", None, None, None)
    return jax.shard_map(body, mesh=mesh, in_specs=in_specs, out_specs=out_specs, check_vma=False)
```

```python
import functools
import math

import jax
import jax.numpy as jnp
from jax import lax
from jax.experimental import pallas as pl
from jax.experimental.pallas import tpu as pltpu
from jax.sharding import PartitionSpec as P

SUBC = 2
F32 = jnp.float32
BF16 = jnp.bfloat16

soft_near = 0.05
soft_far = 1.0
middle = 0.5


def swap(block, axis, odd):
    count = lax.axis_size(axis)
    pairs = []
    for low in range(odd, count, 2):
        high = (low + 1) % count
        pairs += [(low, high), (high, low)]
    return lax.ppermute(block, axis, pairs)


def exchange(values, axis, step):
    return lax.ppermute(values, axis, [(i, i ^ step) for i in range(lax.axis_size(axis))])


def split_slots(slots, together):
    groups = slots // together
    cuts = [0, max(1, groups // 2), groups]
    return [(a * together, (b - a) * together) for a, b in zip(cuts, cuts[1:]) if b > a]


def near_cost(slots, entries, width):
    pairs = slots * entries * width * width
    return pl.CostEstimate(flops=20 * pairs, bytes_accessed=3 * slots * width * 4, transcendentals=pairs)


def split3(v):
    high = v.astype(BF16).astype(F32)
    rest = v - high
    mid = rest.astype(BF16).astype(F32)
    return high, mid, rest - mid


def roll(v, step):
    return pltpu.roll(v, step, 0)


def halves(low_half, pairs):
    upper, lower = [], []
    for (first, first_rolled), second in pairs:
        second, second_rolled = second or (jnp.zeros_like(first),) * 2
        upper.append(jnp.where(low_half, first, second_rolled))
        lower.append(jnp.where(low_half, first_rolled, second))
    return upper, lower


def rows16(tiles):
    return jnp.concatenate(tiles, axis=0).astype(BF16)


def with_rolled(v):
    return v, roll(v, 4)


def masked(is_mass, value, pair):
    return tuple(jnp.where(is_mass, value, v) for v in pair)


def square_norm(is_mass, centred):
    square = jnp.where(is_mass, 0.0, centred)
    square = square * square
    square = square + roll(square, 1)
    return square + roll(square, 2)


def source_tile(tile, moved, is_mass, low_half):
    centred = (tile + moved) - jnp.where(is_mass, 0.0, middle)
    rows = jnp.where(is_mass, square_norm(is_mass, centred), -2.0 * centred)
    high, mid, low = map(with_rolled, split3(rows))
    high_1, mid_1 = masked(is_mass, 1.0, high), masked(is_mass, 1.0, mid)
    features = halves(low_half, [(high, high_1), (high_1, mid), (mid_1, low)])
    zero = jnp.zeros_like(tile)
    mass = jnp.where(is_mass, tile, 0.0)
    mass = mass + roll(mass, 7)
    mass = mass + roll(mass, 6)
    high, mid, low = map(with_rolled, split3(jnp.where(is_mass, 1.0, centred) * mass))
    moments = halves(low_half, [(high, mid), (low, None)])
    return [rows16([*v, zero]) for v in features], [rows16(v) for v in moments]


def target_tile(tile, is_mass, low_half):
    centred = tile - middle
    norm = square_norm(is_mass, centred) + soft_near * soft_near
    high, mid, low = map(with_rolled, split3(jnp.where(is_mass, norm, centred)))
    one_high = masked(is_mass, 1.0, high)
    high_mid = tuple(jnp.where(is_mass, a, b) for a, b in zip(high, mid))
    mid_low = tuple(jnp.where(is_mass, a, b) for a, b in zip(mid, low))
    low_mid = tuple(jnp.where(is_mass, a, b) for a, b in zip(low, mid))
    groups = halves(low_half, [(one_high, high_mid), (mid_low, one_high), (low_mid, one_high)])
    return [rows16([*v, jnp.zeros_like(tile)]) for v in groups]


def mark(blocks, ids_in, out, ids, sems, *, half_gy):
    rows, width = blocks.shape
    copies = [
        pltpu.make_async_copy(ids_in, ids, sems.at[0]),
        pltpu.make_async_copy(blocks, out.at[pl.ds(0, rows), :], sems.at[1]),
    ]
    for copy in copies:
        copy.start()
    for copy in copies:
        copy.wait()
    first = (lax.axis_index("gx") // 2 * half_gy + lax.axis_index("gy") // 2) * SUBC
    count = ids.shape[1]
    line = lax.broadcasted_iota(jnp.int32, (8, count), 0)
    member = jnp.where(ids[...] - first == line, 1.0, 0.0)
    mass = out[pl.ds(3, count, stride=4), :]
    sums = jnp.dot(member, mass, preferred_element_type=F32, precision=lax.Precision.HIGHEST)
    sums = jnp.sum(sums, axis=1, keepdims=True)
    shape = (out.shape[0] - rows, width)
    cell = lax.broadcasted_iota(jnp.int32, shape, 0) * width + lax.broadcasted_iota(jnp.int32, shape, 1)
    values = jnp.zeros(shape, F32)
    for h in range(SUBC):
        values = jnp.where(cell == first + h, jnp.broadcast_to(sums[h : h + 1], shape), values)
    out[rows:, :] = values


def add_sources(pieces, places, feature, moment, count_blocks):
    width = feature.shape[2]
    even_x, even_y = 1 - lax.axis_index("gx") % 2, 1 - lax.axis_index("gy") % 2
    line = lax.broadcasted_iota(jnp.int32, (8, width), 0)
    is_mass, low_half = line % 4 == 3, line < 4
    is_x, is_y = line % 4 == 0, line % 4 == 1
    tiles = count_blocks // 2
    unroll = math.gcd(tiles, 16)
    for piece, (row, col) in zip(pieces, places):
        a = (1, 2 * even_x, 2 - 2 * even_x)[row]
        b = (1, 2 * even_y, 2 - 2 * even_y)[col]
        step_a = jnp.asarray(a - 1, F32)
        step_b = jnp.asarray(b - 1, F32)
        moved = jnp.where(is_x, step_a, jnp.where(is_y, step_b, 0.0))

        def some_tiles(group, carry, piece=piece, base=(3 * a + b) * tiles, moved=moved):
            for u in range(unroll):
                at = group * unroll + u
                tile = piece[pl.ds(pl.multiple_of(at * 8, 8), 8), :]
                features, moments = source_tile(tile, moved, is_mass, low_half)
                for half in range(2):
                    feature[2 * (base + at) + half] = features[half]
                    moment[2 * (base + at) + half] = moments[half]
            return carry

        lax.fori_loop(0, tiles // unroll, some_tiles, 0)


def start_rows(*refs, places, count_blocks):
    pieces, (feature, moment, target, centre) = refs[:-4], refs[-4:]
    slots, width = centre.shape[1:]
    own = pieces[0]
    line = lax.broadcasted_iota(jnp.int32, (8, width), 0)
    is_mass, low_half = line % 4 == 3, line < 4

    def one_target(pair, carry):
        tile = own[pl.ds(pl.multiple_of(pair * 8, 8), 8), :]
        for half, value in enumerate(target_tile(tile, is_mass, low_half)):
            target[2 * pair + half] = value
        return carry

    lax.fori_loop(0, slots // 2, one_target, 0)
    for c in range(3):
        centre[c] = own[pl.ds(c, slots, stride=4), :] - middle
    add_sources(pieces, places, feature, moment, count_blocks)


def more_rows(feature_in, moment_in, *refs, places, count_blocks):
    pieces, (feature, moment) = refs[:-2], refs[-2:]
    add_sources(pieces, places, feature, moment, count_blocks)


def last_rows(feature_in, moment_in, *refs, places, count_blocks, here, there):
    pieces, (feature, moment, here_mass, there_mass) = refs[:-4], refs[-4:]
    width = feature.shape[2]
    for row in range(here_mass.shape[0] // width):
        for out, members in ((here_mass, here), (there_mass, there)):
            values = [pieces[k][count_blocks * 4 + row, :] for k in members]
            out[pl.ds(row * width, width)] = functools.reduce(jnp.add, values)
    add_sources(pieces[: len(places)], places, feature, moment, count_blocks)


def pair_sums(first, count, limit, lists, feature, moment, target, centre, out, together):
    entries = lists.shape[0]

    def some_slots(group, carry):
        for u in range(together):
            at = group * together + u
            slot = first + at
            near = target[slot]
            sums = jnp.zeros((moment.shape[1], moment.shape[2]), F32)
            for k in range(0, entries, 2):
                one, two = lists[k, slot], lists[k + 1, slot]
                here = jnp.concatenate([feature[one], feature[two]], axis=1)
                parts = jnp.concatenate([moment[one], moment[two]], axis=1)
                dist_sq = lax.dot_general(here, near, (((0,), (0,)), ((), ())), preferred_element_type=F32)
                inverse = lax.rsqrt(dist_sq)
                weight = inverse * inverse * inverse
                high = weight.astype(BF16)
                low = (weight - high.astype(F32)).astype(BF16)
                sums += jnp.dot(parts, high, preferred_element_type=F32)
                sums += jnp.dot(parts, low, preferred_element_type=F32)
            sums = (sums[0:4] + sums[4:8]) + sums[8:12]
            for c in range(3):
                own = centre[c, pl.ds(slot, 1), :]
                out[c, pl.ds(at, 1), :] = sums[c : c + 1] - own * sums[3:4]
        return carry

    groups = jnp.clip(limit - first + together - 1, 0, count) // together
    lax.fori_loop(0, groups, some_slots, 0)


def near_forces(lists_in, tie, limit, feature, moment, target, centre, out, lists, sem, *, first, together):
    copy = pltpu.make_async_copy(lists_in, lists, sem)
    copy.start()
    limit = jnp.max(limit[...].astype(F32)).astype(jnp.int32)
    copy.wait()
    pair_sums(first, out.shape[1], limit, lists, feature, moment, target, centre, out, together)


def add_far(some_mass, more_mass, limit, centre, *refs, half_gy, total):
    nears, out = refs[:-1], refs[-1]
    slots, width = out.shape[1:]
    corner = (lax.axis_index("gx").astype(F32) + middle, lax.axis_index("gy").astype(F32) + middle, middle)
    position = [centre[c] + corner[c] for c in range(3)]
    far = [jnp.zeros((slots, width), F32)] * 3
    for line in range(-(-total // width)):
        at = pl.ds(line * width, width)
        masses = (some_mass[at] + more_mass[at]).reshape(1, width)
        for cell in range(line * width, min(total, (line + 1) * width)):
            group, sub_cell = divmod(cell, SUBC)
            middle_of = (2.0 * (group // half_gy) + 1, 2.0 * (group % half_gy) + 1, (sub_cell + 0.5) / SUBC)
            offset = [middle_of[c] - position[c] for c in range(3)]
            dist_sq = (offset[0] * offset[0] + offset[1] * offset[1]) + offset[2] * offset[2]
            inverse = lax.rsqrt(dist_sq + soft_far * soft_far)
            lane = cell - line * width
            weight = masses[:, lane : lane + 1] * (inverse * inverse * inverse)
            far = [far[c] + weight * offset[c] for c in range(3)]
    active = lax.broadcasted_iota(jnp.int32, (slots, width), 0) < limit[...]
    for c in range(3):
        near = jnp.concatenate([piece[c] for piece in nears], axis=0)
        out[c] = jnp.where(active, near + far[c], 0.0)


def body(blocks, active_counts, pair_lists, cell_ids):
    count_blocks, width = blocks.shape[2], blocks.shape[4]
    slots, entries = pair_lists.shape[2:]
    half_gy = lax.axis_size("gy") // 2
    total = lax.axis_size("gx") // 2 * half_gy * SUBC
    own = blocks.reshape(count_blocks * 4, width)
    smem = pl.BlockSpec(memory_space=pltpu.SMEM)
    vmem = pl.BlockSpec(memory_space=pltpu.VMEM)

    lines = -(-total // width)
    rows = count_blocks * 4
    hbm = pl.BlockSpec(memory_space=pl.ANY)
    marked = pl.pallas_call(
        functools.partial(mark, half_gy=half_gy),
        out_shape=jax.ShapeDtypeStruct((rows + 8 * -(-lines // 8), width), F32),
        in_specs=[hbm] * 2,
        out_specs=vmem,
        scratch_shapes=[pltpu.VMEM((1, count_blocks), jnp.int32), pltpu.SemaphoreType.DMA((2,))],
        compiler_params=pltpu.CompilerParams(vmem_limit_bytes=2 * 2**20),
    )(own, cell_ids[0])
    lists = pair_lists[0, 0].T

    first_x = swap(marked, "gx", 0)
    second_y = swap(marked, "gy", 1)
    first_y = swap(marked, "gy", 0)
    second_x = swap(lax.optimization_barrier((own, marked))[0], "gx", 1)
    row_params = dict(
        compiler_params=pltpu.CompilerParams(vmem_limit_bytes=16 * 2**20),
        cost_estimate=pl.CostEstimate(flops=1, bytes_accessed=1, transcendentals=0),
    )
    table = list(pl.pallas_call(
        functools.partial(start_rows, places=[(0, 0)], count_blocks=count_blocks),
        out_shape=[
            jax.ShapeDtypeStruct((9 * count_blocks, 32, width), BF16),
            jax.ShapeDtypeStruct((9 * count_blocks, 16, width), BF16),
            jax.ShapeDtypeStruct((slots, 32, width), BF16),
            jax.ShapeDtypeStruct((3, slots, width), F32),
        ],
        in_specs=[vmem],
        out_specs=[vmem] * 4,
        **row_params,
    )(marked))

    second_x = second_x
    first_x = lax.optimization_barrier((first_x, table[3]))[0]
    first_xy = swap(first_x, "gy", 0)
    first_xyy = swap(first_x, "gy", 1)

    table[:2] = pl.pallas_call(
        functools.partial(more_rows, places=[(1, 0), (0, 1), (0, 2)], count_blocks=count_blocks),
        out_shape=table[:2],
        in_specs=[vmem] * 5,
        out_specs=[vmem] * 2,
        input_output_aliases={0: 0, 1: 1},
        **row_params,
    )(*table[:2], first_x, first_y, second_y)

    second_xy = swap(second_x, "gy", 0)
    second_xyy = swap(second_x, "gy", 1)
    more = [first_xy, second_x, second_xy, first_xyy, marked, first_x, first_y, second_y]
    *rows_now, here_mass, there_mass = pl.pallas_call(
        functools.partial(
            last_rows,
            places=[(1, 1), (2, 0), (2, 1), (1, 2)],
            count_blocks=count_blocks,
            here=(0, 4, 5, 6),
            there=(3, 7),
        ),
        out_shape=[*table[:2]] + [jax.ShapeDtypeStruct((lines * width,), F32)] * 2,
        in_specs=[vmem] * (2 + len(more)),
        out_specs=[vmem] * 4,
        input_output_aliases={0: 0, 1: 1},
        **row_params,
    )(*table[:2], *more)
    table = [*rows_now, *table[2:]]
    table[:2] = pl.pallas_call(
        functools.partial(more_rows, places=[(2, 2)], count_blocks=count_blocks),
        out_shape=table[:2],
        in_specs=[vmem] * 3,
        out_specs=[vmem] * 2,
        input_output_aliases={0: 0, 1: 1},
        compiler_params=row_params["compiler_params"],
        cost_estimate=pl.CostEstimate(flops=5 * 10**9, bytes_accessed=1, transcendentals=0),
    )(*table[:2], second_xyy)

    together = math.gcd(slots, 8)
    ranges = split_slots(slots, together)

    def near_part(k, tie):
        first, count = ranges[k]
        return pl.pallas_call(
            functools.partial(near_forces, first=first, together=math.gcd(count, 16)),
            out_shape=jax.ShapeDtypeStruct((3, count, width), F32),
            in_specs=[hbm] * 2 + [vmem] * 5,
            out_specs=vmem,
            scratch_shapes=[pltpu.SMEM((entries, slots), jnp.int32), pltpu.SemaphoreType.DMA],
            compiler_params=pltpu.CompilerParams(vmem_limit_bytes=16 * 2**20),
            cost_estimate=near_cost(count, entries, width),
        )(lists, tie, active_counts, *table)

    if lax.axis_size("gy") == 4:
        values = (here_mass + there_mass) + exchange(there_mass, "gy", 1)
        steps = []
    else:
        values = here_mass
        steps = [("gy", 2 << k) for k in range((lax.axis_size("gy") // 2).bit_length() - 1)]
    steps += [("gx", 2 << k) for k in range((lax.axis_size("gx") // 2).bit_length() - 1)]
    nears, parts = [], (values, jnp.zeros_like(values))
    for k, (axis, step) in enumerate(steps):
        values = lax.optimization_barrier((values, nears[-1] if nears else table[0]))[0]
        other = exchange(values, axis, step)
        parts = (values, other)
        if k >= len(steps) - 2 and len(nears) < len(ranges):
            nears.append(near_part(len(nears), values))
        values = values + other
    while len(nears) < len(ranges):
        nears.append(near_part(len(nears), parts[0]))

    result = pl.pallas_call(
        functools.partial(add_far, half_gy=half_gy, total=total),
        out_shape=jax.ShapeDtypeStruct((3, slots, width), F32),
        in_specs=[vmem] * (4 + len(nears)),
        out_specs=vmem,
        compiler_params=pltpu.CompilerParams(vmem_limit_bytes=12 * 2**20),
    )(*parts, active_counts, table[3], *nears)
    return result.transpose(1, 0, 2)[None, None]


def solution(mesh):
    in_specs = (
        P("gx", "gy", None, None, None),
        P("gx", "gy"),
        P("gx", "gy", None, None),
        P("gx", "gy", None),
    )
    out_specs = P("gx", "gy", None, None, None)
    return jax.shard_map(body, mesh=mesh, in_specs=in_specs, out_specs=out_specs, check_vma=False)
```

```python
import functools
import math

import jax
import jax.numpy as jnp
from jax import lax
from jax.experimental import pallas as pl
from jax.experimental.pallas import tpu as pltpu
from jax.sharding import PartitionSpec as P

SUBC = 2
F32 = jnp.float32
BF16 = jnp.bfloat16

soft_near = 0.05
soft_far = 1.0
middle = 0.5


def swap(block, axis, odd):
    count = lax.axis_size(axis)
    pairs = []
    for low in range(odd, count, 2):
        high = (low + 1) % count
        pairs += [(low, high), (high, low)]
    return lax.ppermute(block, axis, pairs)


def exchange(values, axis, step):
    return lax.ppermute(values, axis, [(i, i ^ step) for i in range(lax.axis_size(axis))])


def split_slots(slots, together):
    groups = slots // together
    cuts = [0, max(1, groups // 2), groups]
    return [(a * together, (b - a) * together) for a, b in zip(cuts, cuts[1:]) if b > a]


def near_cost(slots, entries, width):
    pairs = slots * entries * width * width
    return pl.CostEstimate(flops=20 * pairs, bytes_accessed=3 * slots * width * 4, transcendentals=pairs)


def split3(v):
    high = v.astype(BF16).astype(F32)
    rest = v - high
    mid = rest.astype(BF16).astype(F32)
    return high, mid, rest - mid


def roll(v, step):
    return pltpu.roll(v, step, 0)


def halves(low_half, pairs):
    upper, lower = [], []
    for (first, first_rolled), second in pairs:
        second, second_rolled = second or (jnp.zeros_like(first),) * 2
        upper.append(jnp.where(low_half, first, second_rolled))
        lower.append(jnp.where(low_half, first_rolled, second))
    return upper, lower


def rows16(tiles):
    return jnp.concatenate(tiles, axis=0).astype(BF16)


def with_rolled(v):
    return v, roll(v, 4)


def masked(is_mass, value, pair):
    return tuple(jnp.where(is_mass, value, v) for v in pair)


def square_norm(is_mass, centred):
    square = jnp.where(is_mass, 0.0, centred)
    square = square * square
    square = square + roll(square, 1)
    return square + roll(square, 2)


def source_tile(tile, moved, is_mass, low_half):
    centred = (tile + moved) - jnp.where(is_mass, 0.0, middle)
    rows = jnp.where(is_mass, square_norm(is_mass, centred), -2.0 * centred)
    high, mid, low = map(with_rolled, split3(rows))
    high_1, mid_1 = masked(is_mass, 1.0, high), masked(is_mass, 1.0, mid)
    features = halves(low_half, [(high, high_1), (high_1, mid), (mid_1, low)])
    zero = jnp.zeros_like(tile)
    mass = jnp.where(is_mass, tile, 0.0)
    mass = mass + roll(mass, 7)
    mass = mass + roll(mass, 6)
    high, mid, low = map(with_rolled, split3(jnp.where(is_mass, 1.0, centred) * mass))
    moments = halves(low_half, [(high, mid), (low, None)])
    return [rows16([*v, zero]) for v in features], [rows16(v) for v in moments]


def target_tile(tile, is_mass, low_half):
    centred = tile - middle
    norm = square_norm(is_mass, centred) + soft_near * soft_near
    high, mid, low = map(with_rolled, split3(jnp.where(is_mass, norm, centred)))
    one_high = masked(is_mass, 1.0, high)
    high_mid = tuple(jnp.where(is_mass, a, b) for a, b in zip(high, mid))
    mid_low = tuple(jnp.where(is_mass, a, b) for a, b in zip(mid, low))
    low_mid = tuple(jnp.where(is_mass, a, b) for a, b in zip(low, mid))
    groups = halves(low_half, [(one_high, high_mid), (mid_low, one_high), (low_mid, one_high)])
    return [rows16([*v, jnp.zeros_like(tile)]) for v in groups]


def mark(blocks, ids_in, out, ids, sems, *, half_gy):
    rows, width = blocks.shape
    copies = [
        pltpu.make_async_copy(ids_in, ids, sems.at[0]),
        pltpu.make_async_copy(blocks, out.at[pl.ds(0, rows), :], sems.at[1]),
    ]
    for copy in copies:
        copy.start()
    for copy in copies:
        copy.wait()
    first = (lax.axis_index("gx") // 2 * half_gy + lax.axis_index("gy") // 2) * SUBC
    count = ids.shape[1]
    line = lax.broadcasted_iota(jnp.int32, (8, count), 0)
    member = jnp.where(ids[...] - first == line, 1.0, 0.0)
    mass = out[pl.ds(3, count, stride=4), :]
    sums = jnp.dot(member, mass, preferred_element_type=F32, precision=lax.Precision.HIGHEST)
    sums = jnp.sum(sums, axis=1, keepdims=True)
    shape = (out.shape[0] - rows, width)
    cell = lax.broadcasted_iota(jnp.int32, shape, 0) * width + lax.broadcasted_iota(jnp.int32, shape, 1)
    values = jnp.zeros(shape, F32)
    for h in range(SUBC):
        values = jnp.where(cell == first + h, jnp.broadcast_to(sums[h : h + 1], shape), values)
    out[rows:, :] = values


def add_sources(pieces, places, feature, moment, count_blocks):
    width = feature.shape[2]
    even_x, even_y = 1 - lax.axis_index("gx") % 2, 1 - lax.axis_index("gy") % 2
    line = lax.broadcasted_iota(jnp.int32, (8, width), 0)
    is_mass, low_half = line % 4 == 3, line < 4
    is_x, is_y = line % 4 == 0, line % 4 == 1
    tiles = count_blocks // 2
    unroll = math.gcd(tiles, 8)
    for piece, (row, col) in zip(pieces, places):
        a = (1, 2 * even_x, 2 - 2 * even_x)[row]
        b = (1, 2 * even_y, 2 - 2 * even_y)[col]
        step_a = jnp.asarray(a - 1, F32)
        step_b = jnp.asarray(b - 1, F32)
        moved = jnp.where(is_x, step_a, jnp.where(is_y, step_b, 0.0))

        def some_tiles(group, carry, piece=piece, base=(3 * a + b) * tiles, moved=moved):
            for u in range(unroll):
                at = group * unroll + u
                tile = piece[pl.ds(pl.multiple_of(at * 8, 8), 8), :]
                features, moments = source_tile(tile, moved, is_mass, low_half)
                for half in range(2):
                    feature[2 * (base + at) + half] = features[half]
                    moment[2 * (base + at) + half] = moments[half]
            return carry

        lax.fori_loop(0, tiles // unroll, some_tiles, 0)


def start_rows(*refs, places, count_blocks):
    pieces, (feature, moment, target, centre) = refs[:-4], refs[-4:]
    slots, width = centre.shape[1:]
    own = pieces[0]
    line = lax.broadcasted_iota(jnp.int32, (8, width), 0)
    is_mass, low_half = line % 4 == 3, line < 4

    def one_target(pair, carry):
        tile = own[pl.ds(pl.multiple_of(pair * 8, 8), 8), :]
        for half, value in enumerate(target_tile(tile, is_mass, low_half)):
            target[2 * pair + half] = value
        return carry

    lax.fori_loop(0, slots // 2, one_target, 0)
    for c in range(3):
        centre[c] = own[pl.ds(c, slots, stride=4), :] - middle
    add_sources(pieces, places, feature, moment, count_blocks)


def more_rows(feature_in, moment_in, *refs, places, count_blocks):
    pieces, (feature, moment) = refs[:-2], refs[-2:]
    add_sources(pieces, places, feature, moment, count_blocks)


def last_rows(feature_in, moment_in, *refs, places, count_blocks, here, there):
    pieces, (feature, moment, here_mass, there_mass) = refs[:-4], refs[-4:]
    width = feature.shape[2]
    for row in range(here_mass.shape[0] // width):
        for out, members in ((here_mass, here), (there_mass, there)):
            values = [pieces[k][count_blocks * 4 + row, :] for k in members]
            out[pl.ds(row * width, width)] = functools.reduce(jnp.add, values)
    add_sources(pieces[: len(places)], places, feature, moment, count_blocks)


def pair_sums(first, count, limit, lists, feature, moment, target, centre, out, together):
    entries = lists.shape[0]

    def some_slots(group, carry):
        for u in range(together):
            at = group * together + u
            slot = first + at
            near = target[slot]
            sums = jnp.zeros((moment.shape[1], moment.shape[2]), F32)
            for k in range(0, entries, 2):
                one, two = lists[k, slot], lists[k + 1, slot]
                here = jnp.concatenate([feature[one], feature[two]], axis=1)
                parts = jnp.concatenate([moment[one], moment[two]], axis=1)
                dist_sq = lax.dot_general(here, near, (((0,), (0,)), ((), ())), preferred_element_type=F32)
                inverse = lax.rsqrt(dist_sq)
                weight = inverse * inverse * inverse
                high = weight.astype(BF16)
                low = (weight - high.astype(F32)).astype(BF16)
                sums += jnp.dot(parts, high, preferred_element_type=F32)
                sums += jnp.dot(parts, low, preferred_element_type=F32)
            sums = (sums[0:4] + sums[4:8]) + sums[8:12]
            for c in range(3):
                own = centre[c, pl.ds(slot, 1), :]
                out[c, pl.ds(at, 1), :] = sums[c : c + 1] - own * sums[3:4]
        return carry

    groups = jnp.clip(limit - first + together - 1, 0, count) // together
    lax.fori_loop(0, groups, some_slots, 0)


def near_forces(lists_in, tie, limit, feature, moment, target, centre, out, lists, sem, *, first, together):
    copy = pltpu.make_async_copy(lists_in, lists, sem)
    copy.start()
    limit = jnp.max(limit[...].astype(F32)).astype(jnp.int32)
    copy.wait()
    pair_sums(first, out.shape[1], limit, lists, feature, moment, target, centre, out, together)


def add_far(some_mass, more_mass, limit, centre, *refs, half_gy, total):
    nears, out = refs[:-1], refs[-1]
    slots, width = out.shape[1:]
    corner = (lax.axis_index("gx").astype(F32) + middle, lax.axis_index("gy").astype(F32) + middle, middle)
    position = [centre[c] + corner[c] for c in range(3)]
    far = [jnp.zeros((slots, width), F32)] * 3
    for line in range(-(-total // width)):
        at = pl.ds(line * width, width)
        masses = (some_mass[at] + more_mass[at]).reshape(1, width)
        for cell in range(line * width, min(total, (line + 1) * width)):
            group, sub_cell = divmod(cell, SUBC)
            middle_of = (2.0 * (group // half_gy) + 1, 2.0 * (group % half_gy) + 1, (sub_cell + 0.5) / SUBC)
            offset = [middle_of[c] - position[c] for c in range(3)]
            dist_sq = (offset[0] * offset[0] + offset[1] * offset[1]) + offset[2] * offset[2]
            inverse = lax.rsqrt(dist_sq + soft_far * soft_far)
            lane = cell - line * width
            weight = masses[:, lane : lane + 1] * (inverse * inverse * inverse)
            far = [far[c] + weight * offset[c] for c in range(3)]
    active = lax.broadcasted_iota(jnp.int32, (slots, width), 0) < limit[...]
    for c in range(3):
        near = jnp.concatenate([piece[c] for piece in nears], axis=0)
        out[c] = jnp.where(active, near + far[c], 0.0)


def body(blocks, active_counts, pair_lists, cell_ids):
    count_blocks, width = blocks.shape[2], blocks.shape[4]
    slots, entries = pair_lists.shape[2:]
    half_gy = lax.axis_size("gy") // 2
    total = lax.axis_size("gx") // 2 * half_gy * SUBC
    own = blocks.reshape(count_blocks * 4, width)
    smem = pl.BlockSpec(memory_space=pltpu.SMEM)
    vmem = pl.BlockSpec(memory_space=pltpu.VMEM)

    lines = -(-total // width)
    rows = count_blocks * 4
    hbm = pl.BlockSpec(memory_space=pl.ANY)
    marked = pl.pallas_call(
        functools.partial(mark, half_gy=half_gy),
        out_shape=jax.ShapeDtypeStruct((rows + 8 * -(-lines // 8), width), F32),
        in_specs=[hbm] * 2,
        out_specs=vmem,
        scratch_shapes=[pltpu.VMEM((1, count_blocks), jnp.int32), pltpu.SemaphoreType.DMA((2,))],
        compiler_params=pltpu.CompilerParams(vmem_limit_bytes=2 * 2**20),
    )(own, cell_ids[0])
    lists = pair_lists[0, 0].T

    first_x = swap(marked, "gx", 0)
    second_y = swap(marked, "gy", 1)
    first_y = swap(marked, "gy", 0)
    second_x = swap(lax.optimization_barrier((own, marked))[0], "gx", 1)
    row_params = dict(
        compiler_params=pltpu.CompilerParams(vmem_limit_bytes=16 * 2**20),
        cost_estimate=pl.CostEstimate(flops=1, bytes_accessed=1, transcendentals=0),
    )
    table = list(pl.pallas_call(
        functools.partial(start_rows, places=[(0, 0)], count_blocks=count_blocks),
        out_shape=[
            jax.ShapeDtypeStruct((9 * count_blocks, 32, width), BF16),
            jax.ShapeDtypeStruct((9 * count_blocks, 16, width), BF16),
            jax.ShapeDtypeStruct((slots, 32, width), BF16),
            jax.ShapeDtypeStruct((3, slots, width), F32),
        ],
        in_specs=[vmem],
        out_specs=[vmem] * 4,
        **row_params,
    )(marked))

    second_x = second_x
    first_x = lax.optimization_barrier((first_x, table[3]))[0]
    first_xy = swap(first_x, "gy", 0)
    first_xyy = swap(first_x, "gy", 1)

    table[:2] = pl.pallas_call(
        functools.partial(more_rows, places=[(1, 0), (0, 1), (0, 2)], count_blocks=count_blocks),
        out_shape=table[:2],
        in_specs=[vmem] * 5,
        out_specs=[vmem] * 2,
        input_output_aliases={0: 0, 1: 1},
        **row_params,
    )(*table[:2], first_x, first_y, second_y)

    second_xy = swap(second_x, "gy", 0)
    second_xyy = swap(second_x, "gy", 1)
    more = [first_xy, second_x, second_xy, first_xyy, marked, first_x, first_y, second_y]
    *rows_now, here_mass, there_mass = pl.pallas_call(
        functools.partial(
            last_rows,
            places=[(1, 1), (2, 0), (2, 1), (1, 2)],
            count_blocks=count_blocks,
            here=(0, 4, 5, 6),
            there=(3, 7),
        ),
        out_shape=[*table[:2]] + [jax.ShapeDtypeStruct((lines * width,), F32)] * 2,
        in_specs=[vmem] * (2 + len(more)),
        out_specs=[vmem] * 4,
        input_output_aliases={0: 0, 1: 1},
        **row_params,
    )(*table[:2], *more)
    table = [*rows_now, *table[2:]]
    table[:2] = pl.pallas_call(
        functools.partial(more_rows, places=[(2, 2)], count_blocks=count_blocks),
        out_shape=table[:2],
        in_specs=[vmem] * 3,
        out_specs=[vmem] * 2,
        input_output_aliases={0: 0, 1: 1},
        compiler_params=row_params["compiler_params"],
        cost_estimate=pl.CostEstimate(flops=5 * 10**9, bytes_accessed=1, transcendentals=0),
    )(*table[:2], second_xyy)

    together = math.gcd(slots, 8)
    ranges = split_slots(slots, together)

    def near_part(k, tie):
        first, count = ranges[k]
        return pl.pallas_call(
            functools.partial(near_forces, first=first, together=math.gcd(count, 8 if first else 16)),
            out_shape=jax.ShapeDtypeStruct((3, count, width), F32),
            in_specs=[hbm] * 2 + [vmem] * 5,
            out_specs=vmem,
            scratch_shapes=[pltpu.SMEM((entries, slots), jnp.int32), pltpu.SemaphoreType.DMA],
            compiler_params=pltpu.CompilerParams(vmem_limit_bytes=16 * 2**20),
            cost_estimate=near_cost(count, entries, width),
        )(lists, tie, active_counts, *table)

    if lax.axis_size("gy") == 4:
        values = (here_mass + there_mass) + exchange(there_mass, "gy", 1)
        steps = []
    else:
        values = here_mass
        steps = [("gy", 2 << k) for k in range((lax.axis_size("gy") // 2).bit_length() - 1)]
    steps += [("gx", 2 << k) for k in range((lax.axis_size("gx") // 2).bit_length() - 1)]
    nears, parts = [], (values, jnp.zeros_like(values))
    for k, (axis, step) in enumerate(steps):
        values = lax.optimization_barrier((values, nears[-1] if nears else table[0]))[0]
        other = exchange(values, axis, step)
        parts = (values, other)
        if k >= len(steps) - 2 and len(nears) < len(ranges):
            nears.append(near_part(len(nears), values))
        values = values + other
    while len(nears) < len(ranges):
        nears.append(near_part(len(nears), parts[0]))

    result = pl.pallas_call(
        functools.partial(add_far, half_gy=half_gy, total=total),
        out_shape=jax.ShapeDtypeStruct((3, slots, width), F32),
        in_specs=[vmem] * (4 + len(nears)),
        out_specs=vmem,
        compiler_params=pltpu.CompilerParams(vmem_limit_bytes=12 * 2**20),
    )(*parts, active_counts, table[3], *nears)
    return result.transpose(1, 0, 2)[None, None]


def solution(mesh):
    in_specs = (
        P("gx", "gy", None, None, None),
        P("gx", "gy"),
        P("gx", "gy", None, None),
        P("gx", "gy", None),
    )
    out_specs = P("gx", "gy", None, None, None)
    return jax.shard_map(body, mesh=mesh, in_specs=in_specs, out_specs=out_specs, check_vma=False)
```
